768 devices in a mesh: user: 32 (over x, y_hi, core), item: 24 (over y_lo, z).
Axes of the slice: x: 4, y: 8 (y_hi: 4, y_lo: 2; y = y_hi * 2 + y_lo), z: 12, core: 2. Of those that a mesh axis runs over, the one named last changes fastest.
Arguments:
- tile_index: int32 [32, 24, 48], P('user', 'item'), may hold values from -1 to 1535, as said below
- tile_values: bfloat16 [32, 24, 48, 128, 128], P('user', 'item'), may hold values from 10 to 1000
- w_init: float32 [64, 196608], P(None, ('user', 'item')), may hold values from 0.01 to 20, as said below
- h_init: float32 [64, 98304], P(None, ('item', 'user')), may hold values from 0.0001 to 1, as said below
Outputs:
- w_new: float32 [64, 196608], P(None, ('user', 'item'))
- h_new: float32 [64, 98304], P(None, ('item', 'user'))
The draws below stay inside these ranges and needn't reach their ends.
Inputs may be any that keep to these rules, and one draw needn't show every extreme that they name: `tile_index`: in each block the slots holding a tile come first and the rest hold -1; the tiles of one block are distinct, no two of them among the same 32 consecutive tile numbers; every block holds at least 12 tiles; every slot holds a tile in some block. `w_init`: all entries are positive. `h_init`: all entries are positive.
All inputs are finite; a program needn't handle non-finite values.
Results may differ from the reference program's by a relative error of at most 0.0038.
Values may be sent and summed in bfloat16 or wider, within the bound.
A program may use at most 32 MiB of HBM per device.

```python
import math
import jax
import jax.numpy as jnp
from jax import lax

RANK = 64
TILE = 128
STRIDE = 32
USER_TILES = 48
ITEM_TILES = 32
TILES_DEV = 48
USERS = 196608
ITEMS = 98304
N_USER = 32
N_ITEM = 24


def draw_tile_index(key, part):
    blocks_all = N_USER * N_ITEM
    first, second, third, fourth, fifth = jax.random.split(key, 5)
    stripes = jax.vmap(lambda single: jax.random.permutation(single, TILES_DEV))(jax.random.split(first, blocks_all))
    offsets = jax.random.randint(second, (blocks_all, TILES_DEV), 0, STRIDE)
    tiles = (stripes * STRIDE + offsets).astype(jnp.int32)
    counts = jax.random.randint(third, (blocks_all,), max(1, TILES_DEV // 4), TILES_DEV // 2 + 1)
    filled = jax.random.randint(fourth, (blocks_all,), 0, 8) == 0
    counts = jnp.where(filled, TILES_DEV, counts)
    forced = jax.random.randint(fifth, (), 0, blocks_all)
    counts = jnp.where(jnp.arange(blocks_all) == forced, TILES_DEV, counts)
    slots = jnp.arange(TILES_DEV)
    chosen = jnp.where(slots[None, :] < counts[:, None], tiles, -1)
    return chosen.reshape(N_USER, N_ITEM, TILES_DEV).astype(jnp.int32)


def draw_w_init(key, part):
    first, second, third = jax.random.split(key, 3)
    shape = (RANK, USERS)
    heavy_user = jax.random.bernoulli(first, 1.0 / 16.0, (1, USERS))
    light_part = jnp.exp(jax.random.uniform(second, shape, jnp.float32, jnp.log(0.01), 0.0))
    strong = jnp.exp(jax.random.uniform(third, shape, jnp.float32, jnp.log(8.0), jnp.log(20.0)))
    return jnp.where(heavy_user, strong, light_part).astype(jnp.float32)


def draw_h_init(key, part):
    first, second, third, fourth = jax.random.split(key, 4)
    shape = (RANK, ITEMS)
    active = jax.random.bernoulli(first, 1.0 / 32.0, shape)
    strong = jnp.exp(jax.random.uniform(second, shape, jnp.float32, jnp.log(0.1), 0.0))
    level = jnp.exp(jax.random.uniform(third, (RANK, 1), jnp.float32, jnp.log(0.0001), jnp.log(0.001)))
    spread = jnp.exp(jax.random.uniform(fourth, shape, jnp.float32, 0.0, jnp.log(10.0)))
    weak = level * spread
    return jnp.where(active, strong, weak).astype(jnp.float32)


def steps_of(stream_key, shape, cuts, least, top_value):
    loudness = 1.0
    for axis_at, blocks in cuts:
        draws = jax.random.uniform(jax.random.fold_in(jax.random.fold_in(stream_key, 6), axis_at), (blocks,), jnp.float32, least / len(cuts), top_value / len(cuts))
        loudness = loudness * jnp.repeat(jnp.exp(draws), shape[axis_at] // blocks).reshape((-1,) + (1,) * (len(shape) - 1 - axis_at))
    return loudness


def setup_inputs(seed: int = 0) -> dict:
    seeds = jax.random.split(jax.random.key(seed), 5)
    tile_index = draw_tile_index(jax.random.fold_in(seeds[4], 71), 0)
    tile_values = jnp.clip(jnp.exp(math.log(1000.0) - 4.6051702 * jax.random.uniform(seeds[1], (N_USER, N_ITEM, TILES_DEV, TILE, TILE), jnp.float32) ** steps_of(seeds[1], (N_USER, N_ITEM, TILES_DEV, TILE, TILE), ((0, 32), (1, 24)), -0.2, 0.2)), 10.0, 1000.0).astype(jnp.bfloat16)
    w_init = draw_w_init(jax.random.fold_in(seeds[4], 71), 0)
    h_init = draw_h_init(jax.random.fold_in(seeds[4], 71), 0)
    return {"tile_index": tile_index, "tile_values": tile_values, "w_init": w_init, "h_init": h_init}


floor_value = 1e-4


def hals_sweep(factor, cross, gram):
    def update(column, current):
        gram_row = lax.dynamic_index_in_dim(gram, column, 0, keepdims=False)
        pivot = lax.dynamic_index_in_dim(gram_row, column, 0, keepdims=False)
        old_row = lax.dynamic_index_in_dim(current, column, 0, keepdims=False)
        cross_row = lax.dynamic_index_in_dim(cross, column, 0, keepdims=False)
        fitted = jnp.dot(gram_row, current, precision=lax.Precision.HIGHEST)
        new_row = jnp.maximum(old_row + (cross_row - fitted) / pivot, floor_value)
        return lax.dynamic_update_index_in_dim(current, new_row, column, 0)
    return lax.fori_loop(0, factor.shape[0], update, factor)


def reference(tile_index, tile_values, w_init, h_init):
    rank_size = w_init.shape[0]
    blocks = jnp.arange(N_ITEM, dtype=jnp.int32)[:, None]
    h_half = h_init.astype(jnp.bfloat16)
    gram_h = jnp.dot(h_half, h_half.T, preferred_element_type=jnp.float32)
    h_tiles = h_half.reshape(rank_size, N_ITEM, ITEM_TILES, TILE)

    def user_block(inputs):
        slot_ids, values = inputs
        valid = (slot_ids >= 0).astype(jnp.float32)
        clipped = jnp.maximum(slot_ids, 0).astype(jnp.int32)
        tile_rows = clipped // ITEM_TILES
        tile_cols = clipped % ITEM_TILES
        chosen = h_tiles[:, blocks, tile_cols, :].astype(jnp.float32)
        products = jnp.einsum('kjsi,jsui->jsku', chosen, values.astype(jnp.float32))
        products = products * valid[:, :, None, None]
        summed = jax.ops.segment_sum(products.reshape(-1, rank_size, TILE), tile_rows.reshape(-1), num_segments=USER_TILES)
        return jnp.transpose(summed, (1, 0, 2)).reshape(rank_size, USER_TILES * TILE)

    cross_w = lax.map(user_block, (tile_index, tile_values))
    cross_w = jnp.transpose(cross_w, (1, 0, 2)).reshape(rank_size, -1)
    w_new = hals_sweep(w_init, cross_w, gram_h)
    w_half = w_new.astype(jnp.bfloat16)
    gram_w = jnp.dot(w_half, w_half.T, preferred_element_type=jnp.float32)
    w_tiles = w_half.reshape(rank_size, N_USER, USER_TILES, TILE)

    def item_block(running, inputs):
        block, slot_ids, values = inputs
        valid = (slot_ids >= 0).astype(jnp.float32)
        clipped = jnp.maximum(slot_ids, 0).astype(jnp.int32)
        tile_rows = clipped // ITEM_TILES
        tile_cols = clipped % ITEM_TILES
        own_rows = lax.dynamic_index_in_dim(w_tiles, block, 1, keepdims=False)
        chosen = own_rows[:, tile_rows, :].astype(jnp.float32)
        products = jnp.einsum('kjsu,jsui->jski', chosen, values.astype(jnp.float32))
        products = products * valid[:, :, None, None]
        targets = (blocks * ITEM_TILES + tile_cols).astype(jnp.int32)
        summed = jax.ops.segment_sum(products.reshape(-1, rank_size, TILE), targets.reshape(-1), num_segments=N_ITEM * ITEM_TILES)
        return running + jnp.transpose(summed, (1, 0, 2)).reshape(rank_size, -1), None

    start_sum = jnp.zeros((rank_size, h_init.shape[1]), jnp.float32)
    cross_h, _ = lax.scan(item_block, start_sum, (jnp.arange(N_USER, dtype=jnp.int32), tile_index, tile_values))
    h_new = hals_sweep(h_init, cross_h, gram_w)
    return (w_new, h_new)
```

```python
import functools

import jax
import jax.numpy as jnp
from jax import lax
from jax.experimental import pallas as pl
from jax.experimental.pallas import tpu as pltpu
from jax.sharding import PartitionSpec as P

RANK = 64
TILE = 128
USER_TILES = 48
ITEM_TILES = 32
SLOTS = 48
NX, NYH, NC = 4, 4, 2
NYL, NZ = 2, 12
FLOOR = 0.0001
F32 = jnp.float32
BF16 = jnp.bfloat16
MESH = pl.DeviceIdType.MESH

ROW_SLOT, ROW_VALID, ROW_ITEM = 0, 48, 96
SLOT_ROW, SLOT_VALID, SLOT_PREV = 144, 192, 240
COL_LAST = 288


def place(user):
    return (user % 2) * 16 + user // 2


def table(tile_index):
    t = tile_index.reshape(SLOTS)
    valid = t >= 0
    row = jnp.where(valid, t // ITEM_TILES, -1)
    col = jnp.where(valid, t % ITEM_TILES, -1)
    slot = jnp.arange(SLOTS, dtype=jnp.int32)
    of_row = row[None, :] == jnp.arange(USER_TILES, dtype=jnp.int32)[:, None]
    row_slot = jnp.max(jnp.where(of_row, slot[None, :], 0), axis=1)
    row_valid = jnp.max(of_row.astype(jnp.int32), axis=1)
    row_item = jnp.max(jnp.where(of_row, place(jnp.maximum(col, 0))[None, :], 0), axis=1)
    before = (col[None, :] == col[:, None]) & (slot[None, :] < slot[:, None])
    prev = jnp.max(jnp.where(before, slot[None, :] + 1, 0), axis=1)
    of_col = col[None, :] == jnp.arange(ITEM_TILES, dtype=jnp.int32)[:, None]
    last = jnp.max(jnp.where(of_col, slot[None, :] + 1, 0), axis=1)
    return jnp.concatenate(
        [row_slot, row_valid, row_item, jnp.maximum(row, 0), valid.astype(jnp.int32), prev, last]
    )


def fold(gram):
    return jnp.concatenate([gram[:32, :], gram[32:, :]], axis=1)


def unfold(folded):
    return jnp.concatenate([folded[:, :64], folded[:, 64:]], axis=0)


def dot_t(a, b):
    return lax.dot_general(a, b, (((1,), (1,)), ((), ())), preferred_element_type=F32)


def hals(gram, start_ref, cross, spread, resid, out_ref):
    n = start_ref.shape[1]
    eye = lax.broadcasted_iota(jnp.int32, (RANK, RANK), 0) == lax.broadcasted_iota(
        jnp.int32, (RANK, RANK), 1
    )
    inverse = 1.0 / jnp.sum(jnp.where(eye, gram, 0.0), axis=1, keepdims=True)
    scaled = gram * inverse
    fitted = jnp.dot(gram, start_ref[...], precision=lax.Precision.HIGHEST, preferred_element_type=F32)
    resid[:, :n] = (cross - fitted) * inverse
    for k in range(RANK):
        spread[k] = jnp.broadcast_to(scaled[:, k : k + 1], (RANK, TILE))

    def block(b, _):
        at = pl.multiple_of(b * 8, 8)
        rows = pl.ds(at, 8)
        for lane in range(0, n, TILE):
            r = resid[rows, lane : lane + TILE]
            old = start_ref[rows, lane : lane + TILE]
            deltas = []
            news = []
            for i in range(8):
                new = jnp.maximum(old[i : i + 1] + r[i : i + 1], FLOOR)
                delta = jnp.broadcast_to(new - old[i : i + 1], (8, TILE))
                r = r - spread[b * 8 + i, rows, :] * delta
                deltas.append(delta)
                news.append(new)
            out_ref[rows, lane : lane + TILE] = jnp.concatenate(news, axis=0)
            for j in range(0, RANK, 8):
                acc = resid[j : j + 8, lane : lane + TILE]
                for i in range(8):
                    acc = acc - spread[b * 8 + i, j : j + 8, :] * deltas[i]
                resid[j : j + 8, lane : lane + TILE] = acc
        return 0

    lax.fori_loop(0, RANK // 8, block, 0)


def kernel(
    tab, vals, w_init, h_init, w_out, h_out,
    hbuf, wbuf, acc, ysend, yrecv, zsend, zrecv, gsend, grecv,
    csend, crecv, cgsend, cgrecv, xsend, xrecv, vsend, vrecv, own4, spread, resid,
    hy_s, hy_r, hx_s, hx_r, hc_s, hc_r, ya_s, ya_r, g_s, g_r, z_s, z_r,
    wz_s, wz_r, wy_s, wy_r, c_s, c_r, cg_s, cg_r, x_s, x_r, v_s, v_r,
):
    user = lax.axis_index("user")
    item = lax.axis_index("item")
    x, yh, core = user // 8, (user // 2) % 4, user % 2
    yl, z = item // NZ, item % NZ

    def at_user(x_, yh_, core_):
        return {"user": x_ * 8 + yh_ * 2 + core_, "item": item}

    def at_item(yl_, z_):
        return {"user": user, "item": yl_ * NZ + z_}

    to_y = [at_user(x, (yh + d) % 4, core) for d in range(1, 4)]
    to_x = [at_user((x + d) % 4, yh, core) for d in range(1, 4)]
    to_core = at_user(x, yh, 1 - core)
    to_yl = at_item(1 - yl, z)
    to_z = [at_item(yl, (z + d) % NZ) for d in range(1, NZ)]

    barrier = pltpu.get_barrier_semaphore()
    partners = to_y + to_x + [to_core, to_yl] + to_z
    for partner in partners:
        pl.semaphore_signal(barrier, inc=1, device_id=partner, device_id_type=MESH)
    mine = core * 16 + x * 4 + yh
    hbuf[mine] = h_init[...].astype(BF16)
    acc[0] = jnp.zeros((RANK, TILE), F32)
    pl.semaphore_wait(barrier, len(partners))

    sent = []

    def send(src, dst, s_sem, r_sem, device):
        copy = pltpu.make_async_remote_copy(
            src_ref=src, dst_ref=dst, send_sem=s_sem, recv_sem=r_sem, device_id=device, device_id_type=MESH
        )
        copy.start()
        sent.append(copy)
        return copy

    ys = [send(hbuf.at[mine], hbuf.at[mine], hy_s.at[d], hy_r.at[d], to_y[d]) for d in range(3)]
    for copy in ys:
        copy.wait_recv()
    line = pl.ds(core * 16 + x * 4, 4)
    xs = [send(hbuf.at[line], hbuf.at[line], hx_s.at[d], hx_r.at[d], to_x[d]) for d in range(3)]
    for copy in xs:
        copy.wait_recv()
    side = pl.ds(core * 16, 16)
    send(hbuf.at[side], hbuf.at[side], hc_s.at[0], hc_r.at[0], to_core).wait_recv()

    def gram_h(p, total):
        for q in range(4):
            part = hbuf[p * 4 + q]
            total = total + dot_t(part, part)
        return total

    gram = fold(lax.fori_loop(0, 8, gram_h, jnp.zeros((RANK, RANK), F32)))
    gsend[...] = gram
    g_copy = send(gsend, grecv, g_s.at[0], g_r.at[0], to_yl)

    def product(row):
        slot = tab[ROW_SLOT + row]
        weight = tab[ROW_VALID + row].astype(F32)
        return dot_t(hbuf[tab[ROW_ITEM + row]], vals[slot]) * weight

    y_copies = []
    for d in range(NZ):
        row = 2 * ((1 - yl) * NZ + (z + d) % NZ)
        ysend[d, :TILE // 2, :] = product(row).astype(BF16)
        ysend[d, TILE // 2 :, :] = product(row + 1).astype(BF16)
        y_copies.append(send(ysend.at[d], yrecv.at[d], ya_s.at[d], ya_r.at[d], to_yl))
    g_copy.wait_recv()
    gram = gram + grecv[...]
    gram_half = gram.astype(BF16)
    z_copies = []
    for d in list(range(1, NZ)) + [0]:
        row = 2 * (yl * NZ + (z + d) % NZ)
        first = product(row)
        second = product(row + 1)
        y_copies[d].wait_recv()
        first = first + yrecv[d, : TILE // 2, :].astype(F32)
        second = second + yrecv[d, TILE // 2 :, :].astype(F32)
        if d:
            zsend[d, :64, :] = first.astype(BF16)
            zsend[d, 64:128, :] = second.astype(BF16)
            zsend[d, 128:160, :] = gram_half
            z_copies.append(send(zsend.at[d], zrecv.at[d], z_s.at[d], z_r.at[d], to_z[d - 1]))
    for d in range(1, NZ):
        z_copies[d - 1].wait_recv()
        first = first + zrecv[d, :64, :].astype(F32)
        second = second + zrecv[d, 64:128, :].astype(F32)
        gram = gram + zrecv[d, 128:160, :].astype(F32)

    hals(unfold(gram), w_init, jnp.concatenate([first, second], axis=1), spread, resid, w_out)

    here = 2 * item
    wbuf[here] = w_out[:, :TILE].astype(BF16)
    wbuf[here + 1] = w_out[:, TILE:].astype(BF16)
    pair = pl.ds(here, 2)
    wz = [send(wbuf.at[pair], wbuf.at[pair], wz_s.at[d], wz_r.at[d], to_z[d - 1]) for d in range(1, NZ)]
    wy = [send(wbuf.at[pair], wbuf.at[pair], wy_s.at[0], wy_r.at[0], to_yl)]
    for d in range(1, NZ):
        wz[d - 1].wait_recv()
        came = pl.ds(2 * (yl * NZ + (z + NZ - d) % NZ), 2)
        wy.append(send(wbuf.at[came], wbuf.at[came], wy_s.at[d], wy_r.at[d], to_yl))
    for copy in wy:
        copy.wait_recv()

    def gram_w(p, total):
        for q in range(4):
            part = wbuf[p * 4 + q]
            total = total + dot_t(part, part)
        return total

    gram = fold(lax.fori_loop(0, 12, gram_w, jnp.zeros((RANK, RANK), F32)))
    cgsend[...] = gram
    cg_copy = send(cgsend, cgrecv, cg_s.at[0], cg_r.at[0], to_core)

    def by_slot(g, _):
        for q in range(8):
            s = g * 8 + q
            part = jnp.dot(wbuf[tab[SLOT_ROW + s]], vals[s], preferred_element_type=F32)
            acc[s + 1] = acc[tab[SLOT_PREV + s]] + part * tab[SLOT_VALID + s].astype(F32)
        return 0

    lax.fori_loop(0, SLOTS // 8, by_slot, 0)

    c_copies = []
    for dx in range(4):
        x_ = (x + dx) % 4
        for y_ in range(4):
            csend[dx, y_] = acc[tab[COL_LAST + x_ * 8 + y_ * 2 + (1 - core)]]
        c_copies.append(send(csend.at[dx], crecv.at[dx], c_s.at[dx], c_r.at[dx], to_core))
    cg_copy.wait_recv()
    gram = gram + cgrecv[...]
    x_copies = []
    for dx in (1, 2, 3, 0):
        x_ = (x + dx) % 4
        c_copies[dx].wait_recv()
        for y_ in range(4):
            total = acc[tab[COL_LAST + x_ * 8 + y_ * 2 + core]] + crecv[dx, y_]
            if dx:
                xsend[dx - 1, y_ * 64 : y_ * 64 + 64, :] = total
            else:
                own4[y_] = total
        if dx:
            xsend[dx - 1, 256:288, :] = gram
            x_copies.append(
                send(xsend.at[dx - 1], xrecv.at[dx - 1], x_s.at[dx - 1], x_r.at[dx - 1], to_x[dx - 1])
            )
    for dx in range(3):
        x_copies[dx].wait_recv()
        for y_ in range(4):
            own4[y_] += xrecv[dx, y_ * 64 : y_ * 64 + 64, :]
        gram = gram + xrecv[dx, 256:288, :]
    v_copies = []
    for dy in range(1, 4):
        vsend[dy - 1, :64, :] = own4[(yh + dy) % 4]
        vsend[dy - 1, 64:96, :] = gram
        v_copies.append(
            send(vsend.at[dy - 1], vrecv.at[dy - 1], v_s.at[dy - 1], v_r.at[dy - 1], to_y[dy - 1])
        )
    cross = own4[yh]
    for dy in range(3):
        v_copies[dy].wait_recv()
        cross = cross + vrecv[dy, :64, :]
        gram = gram + vrecv[dy, 64:96, :]

    hals(unfold(gram), h_init, cross, spread, resid, h_out)
    for copy in sent:
        copy.wait_send()


def shards(tile_index, tile_values, w_init, h_init):
    dma = lambda n: pltpu.SemaphoreType.DMA((n,))
    vmem = pl.BlockSpec(memory_space=pltpu.VMEM)
    return pl.pallas_call(
        kernel,
        out_shape=(
            jax.ShapeDtypeStruct(w_init.shape, F32),
            jax.ShapeDtypeStruct(h_init.shape, F32),
        ),
        in_specs=[pl.BlockSpec(memory_space=pltpu.SMEM), vmem, vmem, vmem],
        out_specs=(vmem, vmem),
        scratch_shapes=[
            pltpu.VMEM((32, RANK, TILE), BF16),
            pltpu.VMEM((48, RANK, TILE), BF16),
            pltpu.VMEM((SLOTS + 1, RANK, TILE), F32),
            pltpu.VMEM((NZ, TILE, TILE), BF16),
            pltpu.VMEM((NZ, TILE, TILE), BF16),
            pltpu.VMEM((NZ, 160, TILE), BF16),
            pltpu.VMEM((NZ, 160, TILE), BF16),
            pltpu.VMEM((32, TILE), F32),
            pltpu.VMEM((32, TILE), F32),
            pltpu.VMEM((4, 4, RANK, TILE), F32),
            pltpu.VMEM((4, 4, RANK, TILE), F32),
            pltpu.VMEM((32, TILE), F32),
            pltpu.VMEM((32, TILE), F32),
            pltpu.VMEM((3, 288, TILE), F32),
            pltpu.VMEM((3, 288, TILE), F32),
            pltpu.VMEM((3, 96, TILE), F32),
            pltpu.VMEM((3, 96, TILE), F32),
            pltpu.VMEM((4, RANK, TILE), F32),
            pltpu.VMEM((RANK, RANK, TILE), F32),
            pltpu.VMEM((RANK, 2 * TILE), F32),
            dma(3), dma(3), dma(3), dma(3), dma(1), dma(1),
            dma(NZ), dma(NZ), dma(1), dma(1), dma(NZ), dma(NZ),
            dma(NZ), dma(NZ), dma(NZ), dma(NZ),
            dma(4), dma(4), dma(1), dma(1), dma(3), dma(3), dma(3), dma(3),
        ],
        compiler_params=pltpu.CompilerParams(
            collective_id=0, has_side_effects=True, vmem_limit_bytes=40 * 2**20
        ),
        name="hals_sweep",
    )(table(tile_index), tile_values[0, 0], w_init, h_init)


def solution(mesh):
    in_specs = (
        P("user", "item", None),
        P("user", "item", None, None, None),
        P(None, ("user", "item")),
        P(None, ("item", "user")),
    )
    out_specs = (P(None, ("user", "item")), P(None, ("item", "user")))
    return jax.shard_map(shards, mesh=mesh, in_specs=in_specs, out_specs=out_specs, check_vma=False)
```

```python
import jax
import jax.numpy as jnp
from jax import lax
from jax.experimental import pallas as pl
from jax.experimental.pallas import tpu as pltpu
from jax.sharding import PartitionSpec as P

RANK = 64
TILE = 128
SLOTS = 48
NYL, NZ = 2, 12
FLOOR = 0.0001
F32 = jnp.float32
BF16 = jnp.bfloat16
I32 = jnp.int32
MESH = pl.DeviceIdType.MESH

Z_ORDER = (6, -5, 5, -4, 4, 2, -2, -3, 3, 1, -1, 0)
Z_RELAY = {6: 3, 5: 2, 4: 1, -5: -2, -4: -1}
W_NEAR = (3, -3, 2, -2, 1, -1)
W_FAR = (4, -4, 5, -5, 6)
W_ORDER = (
    tuple((0, -o) for o in (0,) + W_NEAR)
    + tuple((0, -o) for o in W_FAR)
    + tuple((1, -o) for o in (0,) + W_NEAR)
    + tuple((1, -o) for o in W_FAR)
)


def dot_t(a, b):
    return lax.dot_general(a, b, (((1,), (1,)), ((), ())), preferred_element_type=F32)


def fold(gram):
    return jnp.concatenate([gram[:32, :], gram[32:, :]], axis=1)


def unfold(folded):
    return jnp.concatenate([folded[:, :64], folded[:, 64:]], axis=0)


def hals(gram, start_ref, cross, spread, resid, out_ref):
    n = start_ref.shape[1]
    eye = lax.broadcasted_iota(I32, (RANK, RANK), 0) == lax.broadcasted_iota(I32, (RANK, RANK), 1)
    inverse = 1.0 / jnp.sum(jnp.where(eye, gram, 0.0), axis=1, keepdims=True)
    scaled = gram * inverse
    fitted = jnp.dot(gram, start_ref[...], precision=lax.Precision.HIGHEST, preferred_element_type=F32)
    resid[:, :n] = (cross - fitted) * inverse
    for k in range(RANK):
        spread[k] = jnp.broadcast_to(scaled[:, k : k + 1], (RANK, TILE))

    def block(b, _):
        rows = pl.ds(pl.multiple_of(b * 8, 8), 8)
        for lane in range(0, n, TILE):
            r = resid[rows, lane : lane + TILE]
            old = start_ref[rows, lane : lane + TILE]
            deltas = []
            news = []
            for i in range(8):
                new = jnp.maximum(old[i : i + 1] + r[i : i + 1], FLOOR)
                delta = jnp.broadcast_to(new - old[i : i + 1], (8, TILE))
                r = r - spread[b * 8 + i, rows, :] * delta
                deltas.append(delta)
                news.append(new)
            out_ref[rows, lane : lane + TILE] = jnp.concatenate(news, axis=0)
            for j in range(0, RANK, 8):
                acc = resid[j : j + 8, lane : lane + TILE]
                for i in range(8):
                    acc = acc - spread[b * 8 + i, j : j + 8, :] * deltas[i]
                resid[j : j + 8, lane : lane + TILE] = acc
        return 0

    lax.fori_loop(0, RANK // 8, block, 0)


def kernel(
    tidx, vals_in, w_in, h_in, w_out, h_out,
    vals, w_init, h_init, hbuf, wbuf, acc, ysend, yrecv, zsend, zrecv, gsend, grecv,
    csend, crecv, xsend, xrecv, vsend, vrecv, own4, gsum, ghalf, cgrecv, gxrecv, gyrecv,
    spread, resid, tabv, rows_tab, cols_tab,
    in_sem, hy_s, hy_r, hx_s, hx_r, hc_s, hc_r, ya_s, ya_r, g_s, g_r, z_s, z_r,
    wz_s, wz_r, wy_s, wy_r, c_s, c_r, cg_s, cg_r, gx_s, gx_r, gy_s, gy_r, gc_s, gc_r, x_s, x_r, v_s, v_r,
):
    user = lax.axis_index("user")
    item = lax.axis_index("item")
    x, yh, core = user // 8, (user // 2) % 4, user % 2
    yl, z = item // NZ, item % NZ

    def at_user(x_, yh_, core_):
        return {"user": x_ * 8 + yh_ * 2 + core_, "item": item}

    def z_at(o):
        return lax.rem(z + (o + NZ), NZ)

    to_y = {d: at_user(x, (yh + d) % 4, core) for d in (2, 1, 3)}
    to_x = {d: at_user((x + d) % 4, yh, core) for d in (2, 1, 3)}
    to_core = at_user(x, yh, 1 - core)
    to_yl = {"user": user, "item": (1 - yl) * NZ + z}
    to_z = {o: {"user": user, "item": yl * NZ + z_at(o)} for o in W_NEAR}

    h_copy = pltpu.make_async_copy(h_in, h_init, in_sem.at[0])
    h_copy.start()
    barrier = pltpu.get_barrier_semaphore()
    partners = [to_core, to_yl] + list(to_y.values()) + list(to_x.values()) + list(to_z.values())
    for partner in partners:
        pl.semaphore_signal(barrier, inc=1, device_id=partner, device_id_type=MESH)
    w_copy = pltpu.make_async_copy(w_in, w_init, in_sem.at[1])
    w_copy.start()
    v_copy = pltpu.make_async_copy(vals_in, vals, in_sem.at[2])
    v_copy.start()
    h_copy.wait()

    def spot(dx, dy):
        return core * 16 + ((x + 4 - dx) % 4) * 4 + (yh + 4 - dy) % 4

    mine = spot(0, 0)
    hbuf[mine] = h_init[...].astype(BF16)
    pl.semaphore_wait(barrier, len(partners))

    sent = []

    def send(src, dst, s_sem, r_sem, device):
        copy = pltpu.make_async_remote_copy(
            src_ref=src, dst_ref=dst, send_sem=s_sem, recv_sem=r_sem, device_id=device, device_id_type=MESH
        )
        copy.start()
        sent.append(copy)
        return copy

    def pass_h(at, s_sem, r_sem, device):
        return send(hbuf.at[at], hbuf.at[at], s_sem, r_sem, device)

    h_y = {d: pass_h(mine, hy_s.at[d - 1], hy_r.at[d - 1], to_y[d]) for d in (2, 1, 3)}
    h_x = {}
    h_c = {}

    def on_x(dy):
        at = spot(0, dy)
        for dx in (2, 1, 3):
            n = (dx - 1) * 4 + dy
            h_x[dx, dy] = pass_h(at, hx_s.at[n], hx_r.at[n], to_x[dx])
        h_c[0, dy] = pass_h(at, hc_s.at[dy], hc_r.at[dy], to_core)

    on_x(0)

    lane = lax.broadcasted_iota(I32, (8, TILE), 1)
    slot_of = jnp.zeros((8, TILE), I32)
    col_of = jnp.full((8, TILE), -1, I32)
    for s in range(SLOTS):
        tile = tidx[s]
        hit = lane == lax.shift_right_arithmetic(tile, 5)
        slot_of = jnp.where(hit, s, slot_of)
        col_of = jnp.where(hit, lax.bitwise_and(tile, 31), col_of)
    tabv[0, 0:8, :] = slot_of
    tabv[0, 8:16, :] = col_of
    rows_copy = pltpu.make_async_copy(tabv.at[0], rows_tab, in_sem.at[3])
    rows_copy.start()
    rows_copy.wait()

    def slot_at(row):
        return rows_tab[0, row]

    def col_at(row):
        return rows_tab[8, row]

    def chunk(far, o):
        return (1 - yl if far else yl) * NZ + z_at(o)

    order = [(2 * chunk(far, o) + half) for far, o in W_ORDER for half in (0, 1)]
    cols = [col_at(row) for row in order]
    placed = jnp.full((8, TILE), -1, I32)
    for p, col in enumerate(cols):
        placed = jnp.where(lane == p, col, placed)
    prev = jnp.zeros((8, TILE), I32)
    last = jnp.zeros((8, TILE), I32)
    for p, col in enumerate(cols):
        prev = jnp.where((placed == col) & (lane > p) & (placed >= 0), p + 1, prev)
        last = jnp.where(lane == col, p + 1, last)
    tabv[1, 0:8, :] = prev
    tabv[1, 8:16, :] = last
    cols_copy = pltpu.make_async_copy(tabv.at[1], cols_tab, in_sem.at[4])
    cols_copy.start()
    cols_copy.wait()

    acc[0] = jnp.zeros((RANK, TILE), F32)

    def self_dot(ref, spots):
        total = None
        for at in spots:
            part = ref[at]
            term = dot_t(part, part)
            total = term if total is None else total + term
        return total

    for dy in (1, 3, 2):
        h_y[dy].wait_recv()
        on_x(dy)
    gram = self_dot(hbuf, [spot(0, dy) for dy in range(4)])
    for dy in (0, 1, 3, 2):
        for dx in (1, 3, 2):
            h_x[dx, dy].wait_recv()
            n = dx * 4 + dy
            h_c[dx, dy] = pass_h(spot(dx, dy), hc_s.at[n], hc_r.at[n], to_core)
        gram = gram + self_dot(hbuf, [spot(dx, dy) for dx in (1, 3, 2)])

    def other(dx, dy):
        return lax.rem(spot(dx, dy) + 16, 32)

    v_copy.wait()
    for dy in (0, 1, 3, 2):
        for dx in (0, 1, 3, 2):
            h_c[dx, dy].wait_recv()
        gram = gram + self_dot(hbuf, [other(dx, dy) for dx in (0, 1, 3, 2)])
    gram = fold(gram)
    gsend[...] = gram
    g_copy = send(gsend, grecv, g_s.at[0], g_r.at[0], to_yl)

    def product(row):
        col = jnp.maximum(col_at(row), 0)
        weight = jnp.where(col_at(row) >= 0, 1.0, 0.0)
        item_at = lax.bitwise_and(col, 1) * 16 + lax.shift_right_logical(col, 1)
        return dot_t(hbuf[item_at], vals[slot_at(row)]) * weight

    y_copies = []
    for i, o in enumerate(Z_ORDER):
        row = 2 * chunk(1, o)
        ysend[i, : TILE // 2, :] = product(row).astype(BF16)
        ysend[i, TILE // 2 :, :] = product(row + 1).astype(BF16)
        y_copies.append(send(ysend.at[i], yrecv.at[i], ya_s.at[i], ya_r.at[i], to_yl))
    g_copy.wait_recv()
    gram = gram + grecv[...]
    gram_half = gram.astype(BF16)

    z_copies = {}
    at_of = {o: i for i, o in enumerate(Z_ORDER)}
    for i, o in enumerate(Z_ORDER):
        row = 2 * chunk(0, o)
        first = product(row)
        second = product(row + 1)
        y_copies[i].wait_recv()
        first = first + yrecv[i, :64, :].astype(F32)
        second = second + yrecv[i, 64:, :].astype(F32)
        if o == 0:
            break
        part_gram = gram
        if abs(o) == 3:
            for far in [f for f in Z_RELAY if f * o > 0]:
                z_copies[far].wait_recv()
                j = at_of[far]
                first = first + zrecv[j, :64, :].astype(F32)
                second = second + zrecv[j, 64:128, :].astype(F32)
                part_gram = part_gram + zrecv[j, 128:160, :].astype(F32)
        zsend[i, :64, :] = first.astype(BF16)
        zsend[i, 64:128, :] = second.astype(BF16)
        zsend[i, 128:160, :] = part_gram.astype(BF16) if abs(o) == 3 else gram_half
        z_copies[o] = send(zsend.at[i], zrecv.at[i], z_s.at[i], z_r.at[i], to_z[Z_RELAY.get(o, o)])
    for o in (2, -2, 1, -1, -3, 3):
        z_copies[o].wait_recv()
        j = at_of[o]
        first = first + zrecv[j, :64, :].astype(F32)
        second = second + zrecv[j, 64:128, :].astype(F32)
        gram = gram + zrecv[j, 128:160, :].astype(F32)

    w_copy.wait()
    hals(unfold(gram), w_init, jnp.concatenate([first, second], axis=1), spread, resid, w_out)

    here = 2 * item
    wbuf[here] = w_out[:, :TILE].astype(BF16)
    wbuf[here + 1] = w_out[:, TILE:].astype(BF16)

    def pass_w(o, s_sem, r_sem, device):
        rows = pl.ds(2 * chunk(0, o), 2)
        return send(wbuf.at[rows], wbuf.at[rows], s_sem, r_sem, device)

    w_y = []

    def over(o):
        n = len(w_y)
        w_y.append(pass_w(o, wy_s.at[n], wy_r.at[n], to_yl))

    w_z = {o: pass_w(0, wz_s.at[n], wz_r.at[n], to_z[o]) for n, o in enumerate(W_NEAR)}
    over(0)
    for o in W_NEAR:
        w_z[o].wait_recv()
        if abs(o) == 3:
            for far in [f for f in W_FAR if f * o > 0]:
                n = 6 + W_FAR.index(far)
                w_z[far] = pass_w(-o, wz_s.at[n], wz_r.at[n], to_z[far - o])
        over(-o)

    gram_w = [jnp.zeros((RANK, RANK), F32)]

    def work(p):
        far, o = W_ORDER[p]
        for half in (0, 1):
            row = 2 * chunk(far, o) + half
            factors = wbuf[row]
            weight = jnp.where(col_at(row) >= 0, 1.0, 0.0)
            part = jnp.dot(factors, vals[slot_at(row)], preferred_element_type=F32) * weight
            acc[2 * p + half + 1] = acc[cols_tab[0, 2 * p + half]] + part
            gram_w[0] = gram_w[0] + dot_t(factors, factors)

    for p in range(7):
        work(p)
    for o in W_FAR:
        w_z[o].wait_recv()
        over(-o)
    for p in range(7, 12):
        work(p)
    for p in range(12, 24):
        w_y[p - 12].wait_recv()
        work(p)

    half_here = pl.ds(pl.multiple_of(core * 16, 16), 16)
    half_there = pl.ds(pl.multiple_of((1 - core) * 16, 16), 16)
    gsum[...] = fold(gram_w[0])
    cg_copy = send(gsum.at[half_there], cgrecv, cg_s.at[0], cg_r.at[0], to_core)

    def column(dx, dy, core_):
        return acc[cols_tab[8, ((x + dx) % 4) * 8 + ((yh + dy) % 4) * 2 + core_]]

    y_order = (2, 1, 3, 0)
    c_copies = {}
    for dy in y_order:
        for dx in range(4):
            csend[dy, dx] = column(dx, dy, 1 - core)
        c_copies[dy] = send(csend.at[dy], crecv.at[dy], c_s.at[dy], c_r.at[dy], to_core)
    cg_copy.wait_recv()
    half_sum = gsum[half_here, :] + cgrecv[...]
    ghalf[0] = half_sum
    gx = {d: send(ghalf.at[0], gxrecv.at[d - 1], gx_s.at[d - 1], gx_r.at[d - 1], to_x[d]) for d in (2, 1, 3)}
    x_copies = {}
    for dy in y_order:
        c_copies[dy].wait_recv()
        for dx in (2, 1, 3, 0):
            total = column(dx, dy, core) + crecv[dy, dx]
            if dx:
                n = (dx - 1) * 4 + dy
                xsend[n] = total
                x_copies[dx, dy] = send(xsend.at[n], xrecv.at[n], x_s.at[n], x_r.at[n], to_x[dx])
            else:
                own4[dy] = total
    for d in (1, 3, 2):
        gx[d].wait_recv()
        half_sum = half_sum + gxrecv[d - 1]
    ghalf[1] = half_sum
    gy = {d: send(ghalf.at[1], gyrecv.at[d - 1], gy_s.at[d - 1], gy_r.at[d - 1], to_y[d]) for d in (2, 1, 3)}
    v_copies = {}
    for dy in y_order:
        cross = own4[dy]
        for dx in (1, 3, 2):
            x_copies[dx, dy].wait_recv()
            cross = cross + xrecv[(dx - 1) * 4 + dy]
        if dy:
            vsend[dy - 1] = cross
            v_copies[dy] = send(vsend.at[dy - 1], vrecv.at[dy - 1], v_s.at[dy - 1], v_r.at[dy - 1], to_y[dy])
    for d in (1, 3, 2):
        gy[d].wait_recv()
        half_sum = half_sum + gyrecv[d - 1]
    ghalf[2] = half_sum
    gc = send(ghalf.at[2], ghalf.at[3], gc_s.at[0], gc_r.at[0], to_core)
    for d in (1, 3, 2):
        v_copies[d].wait_recv()
        cross = cross + vrecv[d - 1]
    gc.wait_recv()
    gsum_low = jnp.where(core == 0, half_sum, ghalf[3])
    gsum_high = jnp.where(core == 0, ghalf[3], half_sum)
    gram = jnp.concatenate([gsum_low, gsum_high], axis=0)

    hals(unfold(gram), h_init, cross, spread, resid, h_out)
    for copy in sent:
        copy.wait_send()


def shards(tile_index, tile_values, w_init, h_init):
    dma = lambda n: pltpu.SemaphoreType.DMA((n,))
    vmem = pl.BlockSpec(memory_space=pltpu.VMEM)
    hbm = pl.BlockSpec(memory_space=pl.ANY)
    return pl.pallas_call(
        kernel,
        out_shape=(
            jax.ShapeDtypeStruct(w_init.shape, F32),
            jax.ShapeDtypeStruct(h_init.shape, F32),
        ),
        in_specs=[pl.BlockSpec(memory_space=pltpu.SMEM), hbm, hbm, hbm],
        out_specs=(vmem, vmem),
        scratch_shapes=[
            pltpu.VMEM((SLOTS, TILE, TILE), BF16),
            pltpu.VMEM((RANK, 2 * TILE), F32),
            pltpu.VMEM((RANK, TILE), F32),
            pltpu.VMEM((32, RANK, TILE), BF16),
            pltpu.VMEM((48, RANK, TILE), BF16),
            pltpu.VMEM((SLOTS + 1, RANK, TILE), F32),
            pltpu.VMEM((NZ, TILE, TILE), BF16),
            pltpu.VMEM((NZ, TILE, TILE), BF16),
            pltpu.VMEM((NZ - 1, 160, TILE), BF16),
            pltpu.VMEM((NZ - 1, 160, TILE), BF16),
            pltpu.VMEM((32, TILE), F32),
            pltpu.VMEM((32, TILE), F32),
            pltpu.VMEM((4, 4, RANK, TILE), F32),
            pltpu.VMEM((4, 4, RANK, TILE), F32),
            pltpu.VMEM((12, RANK, TILE), F32),
            pltpu.VMEM((12, RANK, TILE), F32),
            pltpu.VMEM((3, RANK, TILE), F32),
            pltpu.VMEM((3, RANK, TILE), F32),
            pltpu.VMEM((4, RANK, TILE), F32),
            pltpu.VMEM((32, TILE), F32),
            pltpu.VMEM((4, 16, TILE), F32),
            pltpu.VMEM((16, TILE), F32),
            pltpu.VMEM((3, 16, TILE), F32),
            pltpu.VMEM((3, 16, TILE), F32),
            pltpu.VMEM((RANK, RANK, TILE), F32),
            pltpu.VMEM((RANK, 2 * TILE), F32),
            pltpu.VMEM((2, 16, TILE), I32),
            pltpu.SMEM((16, TILE), I32),
            pltpu.SMEM((16, TILE), I32),
            dma(5), dma(3), dma(3), dma(12), dma(12), dma(16), dma(16),
            dma(NZ), dma(NZ), dma(1), dma(1), dma(NZ - 1), dma(NZ - 1),
            dma(11), dma(11), dma(NZ), dma(NZ), dma(4), dma(4), dma(1), dma(1),
            dma(3), dma(3), dma(3), dma(3), dma(1), dma(1), dma(12), dma(12), dma(3), dma(3),
        ],
        compiler_params=pltpu.CompilerParams(
            collective_id=0, has_side_effects=True, vmem_limit_bytes=56 * 2**20
        ),
        name="hals_sweep",
    )(tile_index.reshape(SLOTS), tile_values[0, 0], w_init, h_init)


def solution(mesh):
    in_specs = (
        P("user", "item", None),
        P("user", "item", None, None, None),
        P(None, ("user", "item")),
        P(None, ("item", "user")),
    )
    out_specs = (P(None, ("user", "item")), P(None, ("item", "user")))
    return jax.shard_map(shards, mesh=mesh, in_specs=in_specs, out_specs=out_specs, check_vma=False)
```

```python
import jax
import jax.numpy as jnp
from jax import lax
from jax.experimental import pallas as pl
from jax.experimental.pallas import tpu as pltpu
from jax.sharding import PartitionSpec as P

RANK = 64
TILE = 128
SLOTS = 48
NYL, NZ = 2, 12
FLOOR = 0.0001
F32 = jnp.float32
BF16 = jnp.bfloat16
I32 = jnp.int32
MESH = pl.DeviceIdType.MESH

Z_ORDER = (6, -5, 5, -4, 4, 2, -2, -3, 3, 1, -1, 0)
Z_RELAY = {6: 3, 5: 2, 4: 1, -5: -2, -4: -1}
W_NEAR = (3, -3, 2, -2, 1, -1)
W_FAR = (4, -4, 5, -5, 6)
W_ORDER = (
    tuple((0, -o) for o in (0,) + W_NEAR)
    + tuple((0, -o) for o in W_FAR)
    + tuple((1, -o) for o in (0,) + W_NEAR)
    + tuple((1, -o) for o in W_FAR)
)


def dot_t(a, b):
    return lax.dot_general(a, b, (((1,), (1,)), ((), ())), preferred_element_type=F32)


def fold(gram):
    return jnp.concatenate([gram[:32, :], gram[32:, :]], axis=1)


def unfold(folded):
    return jnp.concatenate([folded[:, :64], folded[:, 64:]], axis=0)


def hals(gram, start_ref, cross, out_ref):
    n = start_ref.shape[1]
    eye = lax.broadcasted_iota(I32, (RANK, RANK), 0) == lax.broadcasted_iota(I32, (RANK, RANK), 1)
    inverse = 1.0 / jnp.sum(jnp.where(eye, gram, 0.0), axis=1, keepdims=True)
    scaled = gram * inverse
    fitted = jnp.dot(gram, start_ref[...], precision=lax.Precision.HIGHEST, preferred_element_type=F32)
    whole = start_ref[...] + (cross - fitted) * inverse
    goal = [whole[j : j + 8, :] for j in range(0, RANK, 8)]
    for b in range(RANK // 8):
        old = start_ref[8 * b : 8 * b + 8, :]
        news = []
        for i in range(8):
            k = 8 * b + i
            new = jnp.maximum(goal[b][i : i + 1, :], FLOOR)
            delta = jnp.broadcast_to(new - old[i : i + 1, :], (8, n))
            for j in range(b, RANK // 8):
                goal[j] = goal[j] - jnp.broadcast_to(scaled[8 * j : 8 * j + 8, k : k + 1], (8, n)) * delta
            news.append(new)
        out_ref[8 * b : 8 * b + 8, :] = jnp.concatenate(news, axis=0)


def kernel(
    tidx, vals_in, w_in, h_in, w_out, h_out,
    vals, w_init, h_init, hbuf, wbuf, acc, ysend, yrecv, zsend, zrecv, gpart, gzrecv,
    csend, crecv, xsend, xrecv, vsend, vrecv, own4, gsum, gsum2, ghalf, cgrecv, gxrecv, gyrecv,
    tabv, rows_tab, cols_tab,
    in_sem, hy_s, hy_r, hx_s, hx_r, hc_s, hc_r, ya_s, ya_r, g_s, g_r, z_s, z_r,
    wz_s, wz_r, wy_s, wy_r, c_s, c_r, cg_s, cg_r, gx_s, gx_r, gy_s, gy_r, gc_s, gc_r, x_s, x_r, v_s, v_r,
):
    user = lax.axis_index("user")
    item = lax.axis_index("item")
    x, yh, core = user // 8, (user // 2) % 4, user % 2
    yl, z = item // NZ, item % NZ

    def at_user(x_, yh_, core_):
        return {"user": x_ * 8 + yh_ * 2 + core_, "item": item}

    def z_at(o):
        return lax.rem(z + (o + NZ), NZ)

    to_y = {d: at_user(x, (yh + d) % 4, core) for d in (2, 1, 3)}
    to_x = {d: at_user((x + d) % 4, yh, core) for d in (2, 1, 3)}
    to_core = at_user(x, yh, 1 - core)
    to_yl = {"user": user, "item": (1 - yl) * NZ + z}
    to_z = {o: {"user": user, "item": yl * NZ + z_at(o)} for o in W_NEAR}

    h_copy = pltpu.make_async_copy(h_in, h_init, in_sem.at[0])
    h_copy.start()
    barrier = pltpu.get_barrier_semaphore()
    partners = [to_y[2], to_z[3], to_z[-3], to_y[1], to_y[3], to_x[2], to_x[1], to_x[3], to_core]
    partners += [to_z[2], to_z[-2], to_z[1], to_z[-1], to_yl]
    for partner in partners:
        pl.semaphore_signal(barrier, inc=1, device_id=partner, device_id_type=MESH)
    w_copy = pltpu.make_async_copy(w_in, w_init, in_sem.at[1])
    w_copy.start()
    v_copy = pltpu.make_async_copy(vals_in, vals, in_sem.at[2])
    v_copy.start()
    h_copy.wait()

    def spot(dx, dy):
        return core * 16 + ((x + 4 - dx) % 4) * 4 + (yh + 4 - dy) % 4

    mine = spot(0, 0)
    hbuf[mine] = h_init[...].astype(BF16)
    lane = lax.broadcasted_iota(I32, (8, TILE), 1)
    slot_of = jnp.zeros((8, TILE), I32)
    col_of = jnp.full((8, TILE), -1, I32)
    for s in range(SLOTS):
        tile = tidx[s]
        hit = lane == lax.shift_right_arithmetic(tile, 5)
        slot_of = jnp.where(hit, s, slot_of)
        col_of = jnp.where(hit, lax.bitwise_and(tile, 31), col_of)
    tabv[0, 0:8, :] = slot_of
    tabv[0, 8:16, :] = col_of
    rows_copy = pltpu.make_async_copy(tabv.at[0], rows_tab, in_sem.at[3])
    rows_copy.start()
    pl.semaphore_wait(barrier, len(partners))

    sent = []

    def drain(keep=0):
        while len(sent) > keep:
            sent.pop(0).wait_send()


    def send(src, dst, s_sem, r_sem, device):
        copy = pltpu.make_async_remote_copy(
            src_ref=src, dst_ref=dst, send_sem=s_sem, recv_sem=r_sem, device_id=device, device_id_type=MESH
        )
        copy.start()
        sent.append(copy)
        return copy

    def pass_h(at, s_sem, r_sem, device):
        return send(hbuf.at[at], hbuf.at[at], s_sem, r_sem, device)

    h_y = {d: pass_h(mine, hy_s.at[d - 1], hy_r.at[d - 1], to_y[d]) for d in (2, 1, 3)}
    h_x = {}
    h_c = {}

    def on_x(dy):
        at = spot(0, dy)
        for dx in (2, 1, 3):
            n = (dx - 1) * 4 + dy
            h_x[dx, dy] = pass_h(at, hx_s.at[n], hx_r.at[n], to_x[dx])
        h_c[0, dy] = pass_h(at, hc_s.at[dy], hc_r.at[dy], to_core)

    on_x(0)

    acc[0] = jnp.zeros((RANK, TILE), F32)

    def self_dot(ref, spots):
        total = None
        for at in spots:
            part = ref[at]
            term = dot_t(part, part)
            total = term if total is None else total + term
        return total

    for dy in (1, 3, 2):
        h_y[dy].wait_recv()
        on_x(dy)

    rows_copy.wait()

    def slot_at(row):
        return rows_tab[0, row]

    def col_at(row):
        return rows_tab[8, row]

    def chunk(far, o):
        return (1 - yl if far else yl) * NZ + z_at(o)

    order = [(2 * chunk(far, o) + half) for far, o in W_ORDER for half in (0, 1)]
    cols = [col_at(row) for row in order]
    placed = jnp.full((8, TILE), -1, I32)
    for p, col in enumerate(cols):
        placed = jnp.where(lane == p, col, placed)
    prev = jnp.zeros((8, TILE), I32)
    last = jnp.zeros((8, TILE), I32)
    for p, col in enumerate(cols):
        prev = jnp.where((placed == col) & (lane > p) & (placed >= 0), p + 1, prev)
        last = jnp.where(lane == col, p + 1, last)
    tabv[1, 0:8, :] = prev
    tabv[1, 8:16, :] = last
    cols_copy = pltpu.make_async_copy(tabv.at[1], cols_tab, in_sem.at[4])
    cols_copy.start()

    gram = self_dot(hbuf, [spot(0, dy) for dy in range(4)])
    for dy in (0, 1, 3, 2):
        for dx in (1, 3, 2):
            h_x[dx, dy].wait_recv()
            n = dx * 4 + dy
            h_c[dx, dy] = pass_h(spot(dx, dy), hc_s.at[n], hc_r.at[n], to_core)
        gram = gram + self_dot(hbuf, [spot(dx, dy) for dx in (1, 3, 2)])

    def other(dx, dy):
        return lax.rem(spot(dx, dy) + 16, 32)

    v_copy.wait()
    cols_copy.wait()
    for dy in (0, 1, 3, 2):
        for dx in (0, 1, 3, 2):
            h_c[dx, dy].wait_recv()
        gram = gram + self_dot(hbuf, [other(dx, dy) for dx in (0, 1, 3, 2)])
    half_here = pl.ds(pl.multiple_of(core * 16, 16), 16)
    half_there = pl.ds(pl.multiple_of((1 - core) * 16, 16), 16)

    gsum[...] = fold(gram)
    part = gsum[half_here, :]
    gpart[0] = part
    at_of = {o: i for i, o in enumerate(Z_ORDER)}
    g_z = {}

    def pass_gram(o, n):
        i = at_of[o]
        g_z[o] = send(gpart.at[n], gzrecv.at[i], g_s.at[i], g_r.at[i], to_z[Z_RELAY.get(o, o)])

    def product(row):
        col = jnp.maximum(col_at(row), 0)
        weight = jnp.where(col_at(row) >= 0, 1.0, 0.0)
        item_at = lax.bitwise_and(col, 1) * 16 + lax.shift_right_logical(col, 1)
        return dot_t(hbuf[item_at], vals[slot_at(row)]) * weight

    y_copies = []
    for i, o in enumerate(Z_ORDER):
        row = 2 * chunk(1, o)
        ysend[i, : TILE // 2, :] = product(row).astype(BF16)
        ysend[i, TILE // 2 :, :] = product(row + 1).astype(BF16)
        y_copies.append(send(ysend.at[i], yrecv.at[i], ya_s.at[i], ya_r.at[i], to_yl))
        for o in ((6, -5, 5), (-4, 4, 2), (-2, 1, -1))[i] if i < 3 else ():
            pass_gram(o, 0)
    for o in (-3, 3):
        through = part
        for far in [f for f in Z_RELAY if Z_RELAY[f] * o > 0]:
            g_z[far].wait_recv()
            through = through + gzrecv[at_of[far]]
        gpart[1 if o > 0 else 2] = through
        pass_gram(o, 1 if o > 0 else 2)

    z_copies = {}

    def pass_z(o, lo, hi, n, device):
        i = at_of[o]
        rows = pl.ds(lo, hi - lo)
        return send(zsend.at[i, rows], zrecv.at[i, rows], z_s.at[n], z_r.at[n], device)

    def came(o, half):
        return zrecv[at_of[o], half * 64 : half * 64 + 64, :].astype(F32)

    for i, o in enumerate(Z_ORDER):
        row = 2 * chunk(0, o)
        first = product(row)
        second = product(row + 1)
        y_copies[i].wait_recv()
        first = first + yrecv[i, :64, :].astype(F32)
        second = second + yrecv[i, 64:, :].astype(F32)
        if o == 0:
            break
        if o == 3:
            z_copies[6].wait_recv()
            first = first + came(6, 0)
        if o == -3:
            z_copies[-6].wait_recv()
            second = second + came(6, 1)
        if abs(o) == 3:
            for far in [f for f in Z_RELAY if f * o > 0 and f != 6]:
                z_copies[far].wait_recv()
                first = first + came(far, 0)
                second = second + came(far, 1)
        zsend[i, :64, :] = first.astype(BF16)
        zsend[i, 64:, :] = second.astype(BF16)
        if o == 6:
            z_copies[6] = pass_z(6, 0, 64, i, to_z[3])
            z_copies[-6] = pass_z(6, 64, 128, NZ - 1, to_z[-3])
        else:
            z_copies[o] = pass_z(o, 0, 128, i, to_z[Z_RELAY.get(o, o)])
        if o == -2:
            for near in (2, -2, 1, -1, -3, 3):
                g_z[near].wait_recv()
                part = part + gzrecv[at_of[near]]
            gpart[3] = part
            g_yl = send(gpart.at[3], gpart.at[4], g_s.at[11], g_r.at[11], to_yl)
        if o == 1:
            g_yl.wait_recv()
            part = part + gpart[4]
            gpart[5] = part
            g_core = send(gpart.at[5], gpart.at[6], g_s.at[12], g_r.at[12], to_core)
    drain(25)
    for o in (2, -2, 1, -1, -3, 3):
        z_copies[o].wait_recv()
        first = first + came(o, 0)
        second = second + came(o, 1)
    g_core.wait_recv()

    def joined(here_, there_):
        return jnp.concatenate([jnp.where(core == 0, here_, there_), jnp.where(core == 0, there_, here_)], axis=0)

    gram = joined(part, gpart[6])

    w_copy.wait()
    hals(unfold(gram), w_init, jnp.concatenate([first, second], axis=1), w_out)

    here = 2 * item
    wbuf[here] = w_out[:, :TILE].astype(BF16)
    wbuf[here + 1] = w_out[:, TILE:].astype(BF16)

    def pass_w(o, s_sem, r_sem, device):
        rows = pl.ds(2 * chunk(0, o), 2)
        return send(wbuf.at[rows], wbuf.at[rows], s_sem, r_sem, device)

    w_y = []

    def over(o):
        n = len(w_y)
        w_y.append(pass_w(o, wy_s.at[n], wy_r.at[n], to_yl))

    over(0)
    w_z = {o: pass_w(0, wz_s.at[n], wz_r.at[n], to_z[o]) for n, o in enumerate(W_NEAR)}
    drain(7)
    for o in W_NEAR:
        w_z[o].wait_recv()
        if abs(o) == 3:
            half, n = (0, 10) if o > 0 else (1, 11)
            row = wbuf.at[2 * chunk(0, -o) + half]
            w_z[2 * o] = send(row, row, wz_s.at[n], wz_r.at[n], to_z[o])
            for far in [f for f in (5, -5, 4, -4) if f * o > 0]:
                n = 6 + W_FAR.index(far)
                w_z[far] = pass_w(-o, wz_s.at[n], wz_r.at[n], to_z[far - o])
        over(-o)

    gram_w = [jnp.zeros((RANK, RANK), F32)]

    def work(p):
        far, o = W_ORDER[p]
        for half in (0, 1):
            row = 2 * chunk(far, o) + half
            factors = wbuf[row]
            weight = jnp.where(col_at(row) >= 0, 1.0, 0.0)
            part = jnp.dot(factors, vals[slot_at(row)], preferred_element_type=F32) * weight
            acc[2 * p + half + 1] = acc[cols_tab[0, 2 * p + half]] + part
            gram_w[0] = gram_w[0] + dot_t(factors, factors)

    for p in range(7):
        work(p)
    for o in W_FAR:
        w_z[o].wait_recv()
        if o == 6:
            w_z[-6].wait_recv()
        over(-o)
    for p in range(7, 12):
        work(p)
    for p in range(12, 24):
        w_y[p - 12].wait_recv()
        work(p)

    gsum2[...] = fold(gram_w[0])
    cg_copy = send(gsum2.at[half_there], cgrecv, cg_s.at[0], cg_r.at[0], to_core)

    def column(dx, dy, core_):
        return acc[cols_tab[8, ((x + dx) % 4) * 8 + ((yh + dy) % 4) * 2 + core_]]

    y_order = (2, 1, 3, 0)
    c_copies = {}
    for dy in y_order:
        for dx in range(4):
            csend[dy, dx] = column(dx, dy, 1 - core)
        c_copies[dy] = send(csend.at[dy], crecv.at[dy], c_s.at[dy], c_r.at[dy], to_core)
    cg_copy.wait_recv()
    half_sum = gsum2[half_here, :] + cgrecv[...]
    ghalf[0] = half_sum
    gx = {d: send(ghalf.at[0], gxrecv.at[d - 1], gx_s.at[d - 1], gx_r.at[d - 1], to_x[d]) for d in (2, 1, 3)}
    x_copies = {}
    for dy in y_order:
        c_copies[dy].wait_recv()
        for dx in (2, 1, 3, 0):
            total = column(dx, dy, core) + crecv[dy, dx]
            if dx:
                n = (dx - 1) * 4 + dy
                xsend[n] = total
                x_copies[dx, dy] = send(xsend.at[n], xrecv.at[n], x_s.at[n], x_r.at[n], to_x[dx])
            else:
                own4[dy] = total
    drain(18)
    for d in (1, 3, 2):
        gx[d].wait_recv()
        half_sum = half_sum + gxrecv[d - 1]
    ghalf[1] = half_sum
    gy = {d: send(ghalf.at[1], gyrecv.at[d - 1], gy_s.at[d - 1], gy_r.at[d - 1], to_y[d]) for d in (2, 1, 3)}
    v_copies = {}
    for dy in y_order:
        cross = own4[dy]
        for dx in (1, 3, 2):
            x_copies[dx, dy].wait_recv()
            cross = cross + xrecv[(dx - 1) * 4 + dy]
        if dy:
            vsend[dy - 1] = cross
            v_copies[dy] = send(vsend.at[dy - 1], vrecv.at[dy - 1], v_s.at[dy - 1], v_r.at[dy - 1], to_y[dy])
    drain(6)
    for d in (1, 3, 2):
        gy[d].wait_recv()
        half_sum = half_sum + gyrecv[d - 1]
    ghalf[2] = half_sum
    gc = send(ghalf.at[2], ghalf.at[3], gc_s.at[0], gc_r.at[0], to_core)
    for d in (1, 3, 2):
        v_copies[d].wait_recv()
        cross = cross + vrecv[d - 1]
    gc.wait_recv()
    gram = joined(half_sum, ghalf[3])

    hals(unfold(gram), h_init, cross, h_out)
    drain()


def shards(tile_index, tile_values, w_init, h_init):
    dma = lambda n: pltpu.SemaphoreType.DMA((n,))
    vmem = pl.BlockSpec(memory_space=pltpu.VMEM)
    hbm = pl.BlockSpec(memory_space=pltpu.HBM)
    return pl.pallas_call(
        kernel,
        out_shape=(
            jax.ShapeDtypeStruct(w_init.shape, F32),
            jax.ShapeDtypeStruct(h_init.shape, F32),
        ),
        in_specs=[pl.BlockSpec(memory_space=pltpu.SMEM), hbm, hbm, hbm],
        out_specs=(vmem, vmem),
        scratch_shapes=[
            pltpu.VMEM((SLOTS, TILE, TILE), BF16),
            pltpu.VMEM((RANK, 2 * TILE), F32),
            pltpu.VMEM((RANK, TILE), F32),
            pltpu.VMEM((32, RANK, TILE), BF16),
            pltpu.VMEM((48, RANK, TILE), BF16),
            pltpu.VMEM((SLOTS + 1, RANK, TILE), F32),
            pltpu.VMEM((NZ, TILE, TILE), BF16),
            pltpu.VMEM((NZ, TILE, TILE), BF16),
            pltpu.VMEM((NZ - 1, TILE, TILE), BF16),
            pltpu.VMEM((NZ - 1, TILE, TILE), BF16),
            pltpu.VMEM((7, 16, TILE), F32),
            pltpu.VMEM((NZ - 1, 16, TILE), F32),
            pltpu.VMEM((4, 4, RANK, TILE), F32),
            pltpu.VMEM((4, 4, RANK, TILE), F32),
            pltpu.VMEM((12, RANK, TILE), F32),
            pltpu.VMEM((12, RANK, TILE), F32),
            pltpu.VMEM((3, RANK, TILE), F32),
            pltpu.VMEM((3, RANK, TILE), F32),
            pltpu.VMEM((4, RANK, TILE), F32),
            pltpu.VMEM((32, TILE), F32),
            pltpu.VMEM((32, TILE), F32),
            pltpu.VMEM((4, 16, TILE), F32),
            pltpu.VMEM((16, TILE), F32),
            pltpu.VMEM((3, 16, TILE), F32),
            pltpu.VMEM((3, 16, TILE), F32),
            pltpu.VMEM((2, 16, TILE), I32),
            pltpu.SMEM((16, TILE), I32),
            pltpu.SMEM((16, TILE), I32),
            dma(5), dma(3), dma(3), dma(12), dma(12), dma(16), dma(16),
            dma(NZ), dma(NZ), dma(13), dma(13), dma(NZ), dma(NZ),
            dma(NZ), dma(NZ), dma(NZ), dma(NZ), dma(4), dma(4), dma(1), dma(1),
            dma(3), dma(3), dma(3), dma(3), dma(1), dma(1), dma(12), dma(12), dma(3), dma(3),
        ],
        compiler_params=pltpu.CompilerParams(
            collective_id=0, has_side_effects=True, vmem_limit_bytes=20 * 2**20
        ),
        name="hals_sweep",
    )(
        tile_index.reshape(SLOTS),
        pltpu.with_memory_space_constraint(tile_values[0, 0], pltpu.HBM),
        pltpu.with_memory_space_constraint(w_init, pltpu.HBM),
        pltpu.with_memory_space_constraint(h_init, pltpu.HBM),
    )


def solution(mesh):
    in_specs = (
        P("user", "item", None),
        P("user", "item", None, None, None),
        P(None, ("user", "item")),
        P(None, ("item", "user")),
    )
    out_specs = (P(None, ("user", "item")), P(None, ("item", "user")))
    return jax.shard_map(shards, mesh=mesh, in_specs=in_specs, out_specs=out_specs, check_vma=False)
```

```python
import jax
import jax.numpy as jnp
from jax import lax
from jax.experimental import pallas as pl
from jax.experimental.pallas import tpu as pltpu
from jax.sharding import PartitionSpec as P

RANK = 64
TILE = 128
SLOTS = 48
NYL, NZ = 2, 12
FLOOR = 0.0001
F32 = jnp.float32
BF16 = jnp.bfloat16
I32 = jnp.int32
MESH = pl.DeviceIdType.MESH

Z_ORDER = (6, -5, 5, -4, 4, 2, -2, -3, 3, 1, -1, 0)
Z_RELAY = {6: 3, 5: 2, 4: 1, -5: -2, -4: -1}
W_NEAR = (3, -3, 2, -2, 1, -1)
W_FAR = (4, -4, 5, -5, 6)
W_ORDER = (
    tuple((0, -o) for o in (0,) + W_NEAR)
    + tuple((0, -o) for o in W_FAR)
    + tuple((1, -o) for o in (0,) + W_NEAR)
    + tuple((1, -o) for o in W_FAR)
)


def dot_t(a, b):
    return lax.dot_general(a, b, (((1,), (1,)), ((), ())), preferred_element_type=F32)


def fold(gram):
    return jnp.concatenate([gram[:32, :], gram[32:, :]], axis=1)


def unfold(folded):
    return jnp.concatenate([folded[:, :64], folded[:, 64:]], axis=0)


def hals(gram, start_ref, cross, out_ref):
    n = start_ref.shape[1]
    eye = lax.broadcasted_iota(I32, (RANK, RANK), 0) == lax.broadcasted_iota(I32, (RANK, RANK), 1)
    inverse = 1.0 / jnp.sum(jnp.where(eye, gram, 0.0), axis=1, keepdims=True)
    scaled = gram * inverse
    fitted = jnp.dot(gram, start_ref[...], precision=lax.Precision.HIGHEST, preferred_element_type=F32)
    whole = start_ref[...] + (cross - fitted) * inverse
    goal = [whole[j : j + 8, :] for j in range(0, RANK, 8)]
    for b in range(RANK // 8):
        old = start_ref[8 * b : 8 * b + 8, :]
        news = []
        for i in range(8):
            k = 8 * b + i
            new = jnp.maximum(goal[b][i : i + 1, :], FLOOR)
            delta = jnp.broadcast_to(new - old[i : i + 1, :], (8, n))
            for j in range(b, RANK // 8):
                goal[j] = goal[j] - jnp.broadcast_to(scaled[8 * j : 8 * j + 8, k : k + 1], (8, n)) * delta
            news.append(new)
        out_ref[8 * b : 8 * b + 8, :] = jnp.concatenate(news, axis=0)


def kernel(
    tidx, vals_in, w_in, h_in, w_out, h_out,
    vals, w_init, h_init, hbuf, wbuf, acc, ysend, yrecv, zsend, zrecv, gpart, gzrecv,
    csend, crecv, xsend, xrecv, vsend, vrecv, own4, gsum, gsum2, ghalf, cgrecv, gxrecv, gyrecv,
    tabv, rows_tab, cols_tab,
    in_sem, hy_s, hy_r, hx_s, hx_r, hc_s, hc_r, ya_s, ya_r, g_s, g_r, z_s, z_r,
    wz_s, wz_r, wy_s, wy_r, c_s, c_r, cg_s, cg_r, gx_s, gx_r, gy_s, gy_r, gc_s, gc_r, x_s, x_r, v_s, v_r,
):
    user = lax.axis_index("user")
    item = lax.axis_index("item")
    x, yh, core = user // 8, (user // 2) % 4, user % 2
    yl, z = item // NZ, item % NZ

    def at_user(x_, yh_, core_):
        return {"user": x_ * 8 + yh_ * 2 + core_, "item": item}

    def z_at(o):
        return lax.rem(z + (o + NZ), NZ)

    to_y = {d: at_user(x, (yh + d) % 4, core) for d in (2, 1, 3)}
    to_x = {d: at_user((x + d) % 4, yh, core) for d in (2, 1, 3)}
    to_core = at_user(x, yh, 1 - core)
    to_yl = {"user": user, "item": (1 - yl) * NZ + z}
    to_z = {o: {"user": user, "item": yl * NZ + z_at(o)} for o in W_NEAR}

    h_copy = pltpu.make_async_copy(h_in, h_init, in_sem.at[0])
    h_copy.start()
    barrier = pltpu.get_barrier_semaphore()
    partners = [to_y[2], to_z[3], to_z[-3], to_y[1], to_y[3], to_x[2], to_x[1], to_x[3], to_core]
    partners += [to_z[2], to_z[-2], to_z[1], to_z[-1], to_yl]
    for partner in partners:
        pl.semaphore_signal(barrier, inc=1, device_id=partner, device_id_type=MESH)
    w_copy = pltpu.make_async_copy(w_in, w_init, in_sem.at[1])
    w_copy.start()
    v_copy = pltpu.make_async_copy(vals_in, vals, in_sem.at[2])
    v_copy.start()
    h_copy.wait()

    def spot(dx, dy):
        return core * 16 + ((x + 4 - dx) % 4) * 4 + (yh + 4 - dy) % 4

    mine = spot(0, 0)
    hbuf[mine] = h_init[...].astype(BF16)
    lane = lax.broadcasted_iota(I32, (8, TILE), 1)
    slot_of = jnp.zeros((8, TILE), I32)
    col_of = jnp.full((8, TILE), -1, I32)
    for s in range(SLOTS):
        tile = tidx[s]
        hit = lane == lax.shift_right_arithmetic(tile, 5)
        slot_of = jnp.where(hit, s, slot_of)
        col_of = jnp.where(hit, lax.bitwise_and(tile, 31), col_of)
    tabv[0, 0:8, :] = slot_of
    tabv[0, 8:16, :] = col_of
    rows_copy = pltpu.make_async_copy(tabv.at[0], rows_tab, in_sem.at[3])
    rows_copy.start()
    pl.semaphore_wait(barrier, len(partners))

    sent = []

    def drain(keep=0):
        while len(sent) > keep:
            sent.pop(0).wait_send()


    def send(src, dst, s_sem, r_sem, device):
        copy = pltpu.make_async_remote_copy(
            src_ref=src, dst_ref=dst, send_sem=s_sem, recv_sem=r_sem, device_id=device, device_id_type=MESH
        )
        copy.start()
        sent.append(copy)
        return copy

    def pass_h(at, s_sem, r_sem, device):
        return send(hbuf.at[at], hbuf.at[at], s_sem, r_sem, device)

    h_y = {d: pass_h(mine, hy_s.at[d - 1], hy_r.at[d - 1], to_y[d]) for d in (2, 1, 3)}
    h_x = {}
    h_c = {}

    def on_x(dy):
        at = spot(0, dy)
        for dx in (2, 1, 3):
            n = (dx - 1) * 4 + dy
            h_x[dx, dy] = pass_h(at, hx_s.at[n], hx_r.at[n], to_x[dx])
        h_c[0, dy] = pass_h(at, hc_s.at[dy], hc_r.at[dy], to_core)

    on_x(0)

    acc[0] = jnp.zeros((RANK, TILE), F32)

    def self_dot(ref, spots):
        total = None
        for at in spots:
            part = ref[at]
            term = dot_t(part, part)
            total = term if total is None else total + term
        return total

    for dy in (1, 3, 2):
        h_y[dy].wait_recv()
        on_x(dy)

    rows_copy.wait()

    def slot_at(row):
        return rows_tab[0, row]

    def col_at(row):
        return rows_tab[8, row]

    def chunk(far, o):
        return (1 - yl if far else yl) * NZ + z_at(o)

    order = [(2 * chunk(far, o) + half) for far, o in W_ORDER for half in (0, 1)]
    cols = [col_at(row) for row in order]
    placed = jnp.full((8, TILE), -1, I32)
    for p, col in enumerate(cols):
        placed = jnp.where(lane == p, col, placed)
    prev = jnp.zeros((8, TILE), I32)
    last = jnp.zeros((8, TILE), I32)
    for p, col in enumerate(cols):
        prev = jnp.where((placed == col) & (lane > p) & (placed >= 0), p + 1, prev)
        last = jnp.where(lane == col, p + 1, last)
    tabv[1, 0:8, :] = prev
    tabv[1, 8:16, :] = last
    cols_copy = pltpu.make_async_copy(tabv.at[1], cols_tab, in_sem.at[4])
    cols_copy.start()

    gram = self_dot(hbuf, [spot(0, dy) for dy in range(4)])
    for dy in (0, 1, 3, 2):
        for dx in (1, 3, 2):
            h_x[dx, dy].wait_recv()
            n = dx * 4 + dy
            h_c[dx, dy] = pass_h(spot(dx, dy), hc_s.at[n], hc_r.at[n], to_core)
        gram = gram + self_dot(hbuf, [spot(dx, dy) for dx in (1, 3, 2)])

    def other(dx, dy):
        return lax.rem(spot(dx, dy) + 16, 32)

    v_copy.wait()
    cols_copy.wait()
    for dy in (0, 1, 3, 2):
        for dx in (0, 1, 3, 2):
            h_c[dx, dy].wait_recv()
        gram = gram + self_dot(hbuf, [other(dx, dy) for dx in (0, 1, 3, 2)])
    half_here = pl.ds(pl.multiple_of(core * 16, 16), 16)
    half_there = pl.ds(pl.multiple_of((1 - core) * 16, 16), 16)

    gsum[...] = fold(gram)
    part = gsum[half_here, :]
    gpart[0] = part
    at_of = {o: i for i, o in enumerate(Z_ORDER)}
    g_z = {}

    def pass_gram(o, n):
        i = at_of[o]
        g_z[o] = send(gpart.at[n], gzrecv.at[i], g_s.at[i], g_r.at[i], to_z[Z_RELAY.get(o, o)])

    def product(row):
        col = jnp.maximum(col_at(row), 0)
        weight = jnp.where(col_at(row) >= 0, 1.0, 0.0)
        item_at = lax.bitwise_and(col, 1) * 16 + lax.shift_right_logical(col, 1)
        return dot_t(hbuf[item_at], vals[slot_at(row)]) * weight

    y_copies = []
    for i, o in enumerate(Z_ORDER):
        row = 2 * chunk(1, o)
        ysend[i, : TILE // 2, :] = product(row).astype(BF16)
        ysend[i, TILE // 2 :, :] = product(row + 1).astype(BF16)
        y_copies.append(send(ysend.at[i], yrecv.at[i], ya_s.at[i], ya_r.at[i], to_yl))
        for o in ((6, -5, 5), (-4, 4, 2), (-2, 1, -1))[i] if i < 3 else ():
            pass_gram(o, 0)
    z_copies = {}

    def pass_z(o, lo, hi, n, device):
        i = at_of[o]
        rows = pl.ds(lo, hi - lo)
        return send(zsend.at[i, rows], zrecv.at[i, rows], z_s.at[n], z_r.at[n], device)

    def came(o, half):
        return zrecv[at_of[o], half * 64 : half * 64 + 64, :].astype(F32)

    for i, o in enumerate(Z_ORDER):
        row = 2 * chunk(0, o)
        first = product(row)
        second = product(row + 1)
        y_copies[i].wait_recv()
        first = first + yrecv[i, :64, :].astype(F32)
        second = second + yrecv[i, 64:, :].astype(F32)
        if o == 0:
            break
        if o == 3:
            z_copies[6].wait_recv()
            first = first + came(6, 0)
        if o == -3:
            z_copies[-6].wait_recv()
            second = second + came(6, 1)
        if abs(o) == 3:
            for far in [f for f in Z_RELAY if f * o > 0 and f != 6]:
                z_copies[far].wait_recv()
                first = first + came(far, 0)
                second = second + came(far, 1)
        zsend[i, :64, :] = first.astype(BF16)
        zsend[i, 64:, :] = second.astype(BF16)
        if o == 6:
            z_copies[6] = pass_z(6, 0, 64, i, to_z[3])
            z_copies[-6] = pass_z(6, 64, 128, NZ - 1, to_z[-3])
        else:
            z_copies[o] = pass_z(o, 0, 128, i, to_z[Z_RELAY.get(o, o)])
        if i == 3:
            for side in (-3, 3):
                through = part
                for far in [f for f in Z_RELAY if Z_RELAY[f] * side > 0]:
                    g_z[far].wait_recv()
                    through = through + gzrecv[at_of[far]]
                gpart[1 if side > 0 else 2] = through
                pass_gram(side, 1 if side > 0 else 2)
        if o == 1:
            for near in (2, -2, 1, -1, -3, 3):
                g_z[near].wait_recv()
                part = part + gzrecv[at_of[near]]
            gpart[3] = part
            g_yl = send(gpart.at[3], gpart.at[4], g_s.at[11], g_r.at[11], to_yl)
    drain(25)
    g_yl.wait_recv()
    part = part + gpart[4]
    gpart[5] = part
    g_core = send(gpart.at[5], gpart.at[6], g_s.at[12], g_r.at[12], to_core)
    for o in (2, -2, 1, -1, -3, 3):
        z_copies[o].wait_recv()
        first = first + came(o, 0)
        second = second + came(o, 1)
    g_core.wait_recv()

    def joined(here_, there_):
        return jnp.concatenate([jnp.where(core == 0, here_, there_), jnp.where(core == 0, there_, here_)], axis=0)

    gram = joined(part, gpart[6])

    w_copy.wait()
    hals(unfold(gram), w_init, jnp.concatenate([first, second], axis=1), w_out)

    here = 2 * item
    wbuf[here] = w_out[:, :TILE].astype(BF16)
    wbuf[here + 1] = w_out[:, TILE:].astype(BF16)

    def pass_w(o, s_sem, r_sem, device):
        rows = pl.ds(2 * chunk(0, o), 2)
        return send(wbuf.at[rows], wbuf.at[rows], s_sem, r_sem, device)

    w_y = []

    def over(o):
        n = len(w_y)
        w_y.append(pass_w(o, wy_s.at[n], wy_r.at[n], to_yl))

    over(0)
    w_z = {o: pass_w(0, wz_s.at[n], wz_r.at[n], to_z[o]) for n, o in enumerate(W_NEAR)}
    drain(7)
    for o in W_NEAR:
        w_z[o].wait_recv()
        if abs(o) == 3:
            half, n = (0, 10) if o > 0 else (1, 11)
            row = wbuf.at[2 * chunk(0, -o) + half]
            w_z[2 * o] = send(row, row, wz_s.at[n], wz_r.at[n], to_z[o])
            for far in [f for f in (5, -5, 4, -4) if f * o > 0]:
                n = 6 + W_FAR.index(far)
                w_z[far] = pass_w(-o, wz_s.at[n], wz_r.at[n], to_z[far - o])
        over(-o)

    gram_w = [jnp.zeros((RANK, RANK), F32)]

    def work(p):
        far, o = W_ORDER[p]
        for half in (0, 1):
            row = 2 * chunk(far, o) + half
            factors = wbuf[row]
            weight = jnp.where(col_at(row) >= 0, 1.0, 0.0)
            part = jnp.dot(factors, vals[slot_at(row)], preferred_element_type=F32) * weight
            acc[2 * p + half + 1] = acc[cols_tab[0, 2 * p + half]] + part
            gram_w[0] = gram_w[0] + dot_t(factors, factors)

    for p in range(7):
        work(p)
    for o in W_FAR:
        w_z[o].wait_recv()
        if o == 6:
            w_z[-6].wait_recv()
        over(-o)
    for p in range(7, 12):
        work(p)
    for p in range(12, 24):
        w_y[p - 12].wait_recv()
        work(p)

    gsum2[...] = fold(gram_w[0])
    cg_copy = send(gsum2.at[half_there], cgrecv, cg_s.at[0], cg_r.at[0], to_core)

    def column(dx, dy, core_):
        return acc[cols_tab[8, ((x + dx) % 4) * 8 + ((yh + dy) % 4) * 2 + core_]]

    y_order = (2, 1, 3, 0)
    c_copies = {}
    for dy in y_order:
        for dx in range(4):
            csend[dy, dx] = column(dx, dy, 1 - core)
        c_copies[dy] = send(csend.at[dy], crecv.at[dy], c_s.at[dy], c_r.at[dy], to_core)
    cg_copy.wait_recv()
    half_sum = gsum2[half_here, :] + cgrecv[...]
    ghalf[0] = half_sum
    gx = {d: send(ghalf.at[0], gxrecv.at[d - 1], gx_s.at[d - 1], gx_r.at[d - 1], to_x[d]) for d in (2, 1, 3)}
    x_copies = {}
    for dy in y_order:
        c_copies[dy].wait_recv()
        for dx in (2, 1, 3, 0):
            total = column(dx, dy, core) + crecv[dy, dx]
            if dx:
                n = (dx - 1) * 4 + dy
                xsend[n] = total
                x_copies[dx, dy] = send(xsend.at[n], xrecv.at[n], x_s.at[n], x_r.at[n], to_x[dx])
            else:
                own4[dy] = total
    drain(18)
    for d in (1, 3, 2):
        gx[d].wait_recv()
        half_sum = half_sum + gxrecv[d - 1]
    ghalf[1] = half_sum
    gy = {d: send(ghalf.at[1], gyrecv.at[d - 1], gy_s.at[d - 1], gy_r.at[d - 1], to_y[d]) for d in (2, 1, 3)}
    v_copies = {}
    for dy in y_order:
        cross = own4[dy]
        for dx in (1, 3, 2):
            x_copies[dx, dy].wait_recv()
            cross = cross + xrecv[(dx - 1) * 4 + dy]
        if dy:
            vsend[dy - 1] = cross
            v_copies[dy] = send(vsend.at[dy - 1], vrecv.at[dy - 1], v_s.at[dy - 1], v_r.at[dy - 1], to_y[dy])
    drain(6)
    for d in (1, 3, 2):
        gy[d].wait_recv()
        half_sum = half_sum + gyrecv[d - 1]
    ghalf[2] = half_sum
    gc = send(ghalf.at[2], ghalf.at[3], gc_s.at[0], gc_r.at[0], to_core)
    for d in (1, 3, 2):
        v_copies[d].wait_recv()
        cross = cross + vrecv[d - 1]
    gc.wait_recv()
    gram = joined(half_sum, ghalf[3])

    hals(unfold(gram), h_init, cross, h_out)
    drain()


def shards(tile_index, tile_values, w_init, h_init):
    dma = lambda n: pltpu.SemaphoreType.DMA((n,))
    vmem = pl.BlockSpec(memory_space=pltpu.VMEM)
    hbm = pl.BlockSpec(memory_space=pltpu.HBM)
    return pl.pallas_call(
        kernel,
        out_shape=(
            jax.ShapeDtypeStruct(w_init.shape, F32),
            jax.ShapeDtypeStruct(h_init.shape, F32),
        ),
        in_specs=[pl.BlockSpec(memory_space=pltpu.SMEM), hbm, hbm, hbm],
        out_specs=(vmem, vmem),
        scratch_shapes=[
            pltpu.VMEM((SLOTS, TILE, TILE), BF16),
            pltpu.VMEM((RANK, 2 * TILE), F32),
            pltpu.VMEM((RANK, TILE), F32),
            pltpu.VMEM((32, RANK, TILE), BF16),
            pltpu.VMEM((48, RANK, TILE), BF16),
            pltpu.VMEM((SLOTS + 1, RANK, TILE), F32),
            pltpu.VMEM((NZ, TILE, TILE), BF16),
            pltpu.VMEM((NZ, TILE, TILE), BF16),
            pltpu.VMEM((NZ - 1, TILE, TILE), BF16),
            pltpu.VMEM((NZ - 1, TILE, TILE), BF16),
            pltpu.VMEM((7, 16, TILE), F32),
            pltpu.VMEM((NZ - 1, 16, TILE), F32),
            pltpu.VMEM((4, 4, RANK, TILE), F32),
            pltpu.VMEM((4, 4, RANK, TILE), F32),
            pltpu.VMEM((12, RANK, TILE), F32),
            pltpu.VMEM((12, RANK, TILE), F32),
            pltpu.VMEM((3, RANK, TILE), F32),
            pltpu.VMEM((3, RANK, TILE), F32),
            pltpu.VMEM((4, RANK, TILE), F32),
            pltpu.VMEM((32, TILE), F32),
            pltpu.VMEM((32, TILE), F32),
            pltpu.VMEM((4, 16, TILE), F32),
            pltpu.VMEM((16, TILE), F32),
            pltpu.VMEM((3, 16, TILE), F32),
            pltpu.VMEM((3, 16, TILE), F32),
            pltpu.VMEM((2, 16, TILE), I32),
            pltpu.SMEM((16, TILE), I32),
            pltpu.SMEM((16, TILE), I32),
            dma(5), dma(3), dma(3), dma(12), dma(12), dma(16), dma(16),
            dma(NZ), dma(NZ), dma(13), dma(13), dma(NZ), dma(NZ),
            dma(NZ), dma(NZ), dma(NZ), dma(NZ), dma(4), dma(4), dma(1), dma(1),
            dma(3), dma(3), dma(3), dma(3), dma(1), dma(1), dma(12), dma(12), dma(3), dma(3),
        ],
        compiler_params=pltpu.CompilerParams(
            collective_id=0, has_side_effects=True, vmem_limit_bytes=20 * 2**20
        ),
        name="hals_sweep",
    )(
        tile_index.reshape(SLOTS),
        pltpu.with_memory_space_constraint(tile_values[0, 0], pltpu.HBM),
        pltpu.with_memory_space_constraint(w_init, pltpu.HBM),
        pltpu.with_memory_space_constraint(h_init, pltpu.HBM),
    )


def solution(mesh):
    in_specs = (
        P("user", "item", None),
        P("user", "item", None, None, None),
        P(None, ("user", "item")),
        P(None, ("item", "user")),
    )
    out_specs = (P(None, ("user", "item")), P(None, ("item", "user")))
    return jax.shard_map(shards, mesh=mesh, in_specs=in_specs, out_specs=out_specs, check_vma=False)
```

```python
import jax
import jax.numpy as jnp
from jax import lax
from jax.experimental import pallas as pl
from jax.experimental.pallas import tpu as pltpu
from jax.sharding import PartitionSpec as P

RANK = 64
TILE = 128
SLOTS = 48
NYL, NZ = 2, 12
FLOOR = 0.0001
F32 = jnp.float32
BF16 = jnp.bfloat16
I32 = jnp.int32
MESH = pl.DeviceIdType.MESH

Z_ORDER = (6, -5, 5, -4, 4, 2, -2, -3, 3, 1, -1, 0)
Z_RELAY = {6: 3, 5: 2, 4: 1, -5: -2, -4: -1}
W_NEAR = (3, -3, 2, -2, 1, -1)
W_FAR = (4, -4, 5, -5, 6)
W_ORDER = (
    tuple((0, -o) for o in (0,) + W_NEAR)
    + tuple((0, -o) for o in W_FAR)
    + tuple((1, -o) for o in (0,) + W_NEAR)
    + tuple((1, -o) for o in W_FAR)
)


def dot_t(a, b):
    return lax.dot_general(a, b, (((1,), (1,)), ((), ())), preferred_element_type=F32)


def fold(gram):
    return jnp.concatenate([gram[:32, :], gram[32:, :]], axis=1)


def unfold(folded):
    return jnp.concatenate([folded[:, :64], folded[:, 64:]], axis=0)


def hals(gram, start_ref, cross, out_ref):
    n = start_ref.shape[1]
    eye = lax.broadcasted_iota(I32, (RANK, RANK), 0) == lax.broadcasted_iota(I32, (RANK, RANK), 1)
    inverse = 1.0 / jnp.sum(jnp.where(eye, gram, 0.0), axis=1, keepdims=True)
    scaled = gram * inverse
    fitted = jnp.dot(gram, start_ref[...], precision=lax.Precision.HIGHEST, preferred_element_type=F32)
    whole = start_ref[...] + (cross - fitted) * inverse
    goal = [whole[j : j + 8, :] for j in range(0, RANK, 8)]
    for b in range(RANK // 8):
        old = start_ref[8 * b : 8 * b + 8, :]
        news = []
        for i in range(8):
            k = 8 * b + i
            new = jnp.maximum(goal[b][i : i + 1, :], FLOOR)
            delta = jnp.broadcast_to(new - old[i : i + 1, :], (8, n))
            for j in range(b, RANK // 8):
                goal[j] = goal[j] - jnp.broadcast_to(scaled[8 * j : 8 * j + 8, k : k + 1], (8, n)) * delta
            news.append(new)
        out_ref[8 * b : 8 * b + 8, :] = jnp.concatenate(news, axis=0)


def kernel(
    tidx, vals_in, w_in, h_in, w_out, h_out,
    vals, w_init, h_init, hbuf, wbuf, acc, ysend, yrecv, zsend, zrecv, gpart, gzrecv,
    csend, crecv, xsend, xrecv, vsend, vrecv, own4, gsum, gsum2, ghalf, cgrecv, gxrecv, gyrecv,
    tabv, rows_tab, cols_tab,
    in_sem, hy_s, hy_r, hx_s, hx_r, hc_s, hc_r, ya_s, ya_r, g_s, g_r, z_s, z_r,
    wz_s, wz_r, wy_s, wy_r, c_s, c_r, cg_s, cg_r, gx_s, gx_r, gy_s, gy_r, gc_s, gc_r, x_s, x_r, v_s, v_r,
):
    user = lax.axis_index("user")
    item = lax.axis_index("item")
    x, yh, core = user // 8, (user // 2) % 4, user % 2
    yl, z = item // NZ, item % NZ

    def at_user(x_, yh_, core_):
        return {"user": x_ * 8 + yh_ * 2 + core_, "item": item}

    def z_at(o):
        return lax.rem(z + (o + NZ), NZ)

    to_y = {d: at_user(x, (yh + d) % 4, core) for d in (2, 1, 3)}
    to_x = {d: at_user((x + d) % 4, yh, core) for d in (2, 1, 3)}
    to_core = at_user(x, yh, 1 - core)
    to_yl = {"user": user, "item": (1 - yl) * NZ + z}
    to_z = {o: {"user": user, "item": yl * NZ + z_at(o)} for o in W_NEAR}

    h_copy = pltpu.make_async_copy(h_in, h_init, in_sem.at[0])
    h_copy.start()
    barrier = pltpu.get_barrier_semaphore()
    partners = [to_y[2], to_z[3], to_z[-3], to_y[1], to_y[3], to_x[2], to_x[1], to_x[3], to_core]
    partners += [to_z[2], to_z[-2], to_z[1], to_z[-1], to_yl]
    for partner in partners:
        pl.semaphore_signal(barrier, inc=1, device_id=partner, device_id_type=MESH)
    w_copy = pltpu.make_async_copy(w_in, w_init, in_sem.at[1])
    w_copy.start()
    v_copy = pltpu.make_async_copy(vals_in, vals, in_sem.at[2])
    v_copy.start()
    h_copy.wait()

    def spot(dx, dy):
        return core * 16 + ((x + 4 - dx) % 4) * 4 + (yh + 4 - dy) % 4

    mine = spot(0, 0)
    hbuf[mine] = h_init[...].astype(BF16)
    lane = lax.broadcasted_iota(I32, (8, TILE), 1)
    slot_of = jnp.zeros((8, TILE), I32)
    col_of = jnp.full((8, TILE), -1, I32)
    for s in range(SLOTS):
        tile = tidx[s]
        hit = lane == lax.shift_right_arithmetic(tile, 5)
        slot_of = jnp.where(hit, s, slot_of)
        col_of = jnp.where(hit, lax.bitwise_and(tile, 31), col_of)
    tabv[0, 0:8, :] = slot_of
    tabv[0, 8:16, :] = col_of
    rows_copy = pltpu.make_async_copy(tabv.at[0], rows_tab, in_sem.at[3])
    rows_copy.start()
    pl.semaphore_wait(barrier, len(partners))

    sent = []

    def drain(keep=0):
        while len(sent) > keep:
            sent.pop(0).wait_send()


    def send(src, dst, s_sem, r_sem, device):
        copy = pltpu.make_async_remote_copy(
            src_ref=src, dst_ref=dst, send_sem=s_sem, recv_sem=r_sem, device_id=device, device_id_type=MESH
        )
        copy.start()
        sent.append(copy)
        return copy

    def pass_h(at, s_sem, r_sem, device):
        return send(hbuf.at[at], hbuf.at[at], s_sem, r_sem, device)

    h_y = {d: pass_h(mine, hy_s.at[d - 1], hy_r.at[d - 1], to_y[d]) for d in (2, 1, 3)}
    h_x = {}
    h_c = {}

    def on_x(dy):
        at = spot(0, dy)
        for dx in (2, 1, 3):
            n = (dx - 1) * 4 + dy
            h_x[dx, dy] = pass_h(at, hx_s.at[n], hx_r.at[n], to_x[dx])
        h_c[0, dy] = pass_h(at, hc_s.at[dy], hc_r.at[dy], to_core)

    on_x(0)

    def slot_at(row):
        return rows_tab[0, row]

    def col_at(row):
        return rows_tab[8, row]

    def chunk(far, o):
        return (1 - yl if far else yl) * NZ + z_at(o)

    acc[0] = jnp.zeros((RANK, TILE), F32)

    def self_dot(ref, spots):
        total = None
        for at in spots:
            part = ref[at]
            term = dot_t(part, part)
            total = term if total is None else total + term
        return total

    for dy in (1, 3, 2):
        h_y[dy].wait_recv()
        on_x(dy)

    for dy in (0, 1, 3, 2):
        for dx in (1, 3, 2):
            h_x[dx, dy].wait_recv()
            n = dx * 4 + dy
            h_c[dx, dy] = pass_h(spot(dx, dy), hc_s.at[n], hc_r.at[n], to_core)

    def other(dx, dy):
        return lax.rem(spot(dx, dy) + 16, 32)

    gram = self_dot(hbuf, [spot(dx, dy) for dx in range(4) for dy in range(4)])
    v_copy.wait()
    rows_copy.wait()
    for dy in (0, 1, 3, 2):
        for dx in (0, 1, 3, 2):
            h_c[dx, dy].wait_recv()
        gram = gram + self_dot(hbuf, [other(dx, dy) for dx in (0, 1, 3, 2)])
    half_here = pl.ds(pl.multiple_of(core * 16, 16), 16)
    half_there = pl.ds(pl.multiple_of((1 - core) * 16, 16), 16)

    gsum[...] = fold(gram)
    part = gsum[half_here, :]
    gpart[0] = part
    at_of = {o: i for i, o in enumerate(Z_ORDER)}
    g_z = {}

    def pass_gram(o, n):
        i = at_of[o]
        g_z[o] = send(gpart.at[n], gzrecv.at[i], g_s.at[i], g_r.at[i], to_z[Z_RELAY.get(o, o)])

    def product(row):
        col = jnp.maximum(col_at(row), 0)
        weight = jnp.where(col_at(row) >= 0, 1.0, 0.0)
        item_at = lax.bitwise_and(col, 1) * 16 + lax.shift_right_logical(col, 1)
        return dot_t(hbuf[item_at], vals[slot_at(row)]) * weight

    y_copies = []
    for i, o in enumerate(Z_ORDER):
        row = 2 * chunk(1, o)
        ysend[i, : TILE // 2, :] = product(row).astype(BF16)
        ysend[i, TILE // 2 :, :] = product(row + 1).astype(BF16)
        y_copies.append(send(ysend.at[i], yrecv.at[i], ya_s.at[i], ya_r.at[i], to_yl))
        for o in ((6, -5, 5), (-4, 4, 2), (-2, 1, -1))[i] if i < 3 else ():
            pass_gram(o, 0)
    order = [(2 * chunk(far, o) + half) for far, o in W_ORDER for half in (0, 1)]
    cols = [col_at(row) for row in order]
    placed = jnp.full((8, TILE), -1, I32)
    for p, col in enumerate(cols):
        placed = jnp.where(lane == p, col, placed)
    prev = jnp.zeros((8, TILE), I32)
    last = jnp.zeros((8, TILE), I32)
    for p, col in enumerate(cols):
        prev = jnp.where((placed == col) & (lane > p) & (placed >= 0), p + 1, prev)
        last = jnp.where(lane == col, p + 1, last)
    tabv[1, 0:8, :] = prev
    tabv[1, 8:16, :] = last
    cols_copy = pltpu.make_async_copy(tabv.at[1], cols_tab, in_sem.at[4])
    cols_copy.start()

    z_copies = {}

    def pass_z(o, lo, hi, n, device):
        i = at_of[o]
        rows = pl.ds(lo, hi - lo)
        return send(zsend.at[i, rows], zrecv.at[i, rows], z_s.at[n], z_r.at[n], device)

    def came(o, half):
        return zrecv[at_of[o], half * 64 : half * 64 + 64, :].astype(F32)

    for i, o in enumerate(Z_ORDER):
        row = 2 * chunk(0, o)
        first = product(row)
        second = product(row + 1)
        y_copies[i].wait_recv()
        first = first + yrecv[i, :64, :].astype(F32)
        second = second + yrecv[i, 64:, :].astype(F32)
        if o == 0:
            break
        if o == 3:
            z_copies[6].wait_recv()
            first = first + came(6, 0)
        if o == -3:
            z_copies[-6].wait_recv()
            second = second + came(6, 1)
        if abs(o) == 3:
            for far in [f for f in Z_RELAY if f * o > 0 and f != 6]:
                z_copies[far].wait_recv()
                first = first + came(far, 0)
                second = second + came(far, 1)
        zsend[i, :64, :] = first.astype(BF16)
        zsend[i, 64:, :] = second.astype(BF16)
        if o == 6:
            z_copies[6] = pass_z(6, 0, 64, i, to_z[3])
            z_copies[-6] = pass_z(6, 64, 128, NZ - 1, to_z[-3])
        else:
            z_copies[o] = pass_z(o, 0, 128, i, to_z[Z_RELAY.get(o, o)])
        if i == 3:
            for side in (-3, 3):
                through = part
                for far in [f for f in Z_RELAY if Z_RELAY[f] * side > 0]:
                    g_z[far].wait_recv()
                    through = through + gzrecv[at_of[far]]
                gpart[1 if side > 0 else 2] = through
                pass_gram(side, 1 if side > 0 else 2)
        if o == 1:
            for near in (2, -2, 1, -1, -3, 3):
                g_z[near].wait_recv()
                part = part + gzrecv[at_of[near]]
            gpart[3] = part
            g_yl = send(gpart.at[3], gpart.at[4], g_s.at[11], g_r.at[11], to_yl)
    drain(25)
    g_yl.wait_recv()
    part = part + gpart[4]
    gpart[5] = part
    g_core = send(gpart.at[5], gpart.at[6], g_s.at[12], g_r.at[12], to_core)
    for o in (2, -2, 1, -1, -3, 3):
        z_copies[o].wait_recv()
        first = first + came(o, 0)
        second = second + came(o, 1)
    g_core.wait_recv()

    def joined(here_, there_):
        return jnp.concatenate([jnp.where(core == 0, here_, there_), jnp.where(core == 0, there_, here_)], axis=0)

    gram = joined(part, gpart[6])

    w_copy.wait()
    hals(unfold(gram), w_init, jnp.concatenate([first, second], axis=1), w_out)

    here = 2 * item
    wbuf[here] = w_out[:, :TILE].astype(BF16)
    wbuf[here + 1] = w_out[:, TILE:].astype(BF16)

    def pass_w(o, s_sem, r_sem, device):
        rows = pl.ds(2 * chunk(0, o), 2)
        return send(wbuf.at[rows], wbuf.at[rows], s_sem, r_sem, device)

    w_y = []

    def over(o):
        n = len(w_y)
        w_y.append(pass_w(o, wy_s.at[n], wy_r.at[n], to_yl))

    over(0)
    w_z = {o: pass_w(0, wz_s.at[n], wz_r.at[n], to_z[o]) for n, o in enumerate(W_NEAR)}
    drain(7)
    for o in W_NEAR:
        w_z[o].wait_recv()
        if abs(o) == 3:
            half, n = (0, 10) if o > 0 else (1, 11)
            row = wbuf.at[2 * chunk(0, -o) + half]
            w_z[2 * o] = send(row, row, wz_s.at[n], wz_r.at[n], to_z[o])
            for far in [f for f in (5, -5, 4, -4) if f * o > 0]:
                n = 6 + W_FAR.index(far)
                w_z[far] = pass_w(-o, wz_s.at[n], wz_r.at[n], to_z[far - o])
        over(-o)

    cols_copy.wait()
    gram_w = [jnp.zeros((RANK, RANK), F32)]

    def work(p):
        far, o = W_ORDER[p]
        for half in (0, 1):
            row = 2 * chunk(far, o) + half
            factors = wbuf[row]
            weight = jnp.where(col_at(row) >= 0, 1.0, 0.0)
            part = jnp.dot(factors, vals[slot_at(row)], preferred_element_type=F32) * weight
            acc[2 * p + half + 1] = acc[cols_tab[0, 2 * p + half]] + part
            gram_w[0] = gram_w[0] + dot_t(factors, factors)

    for p in range(7):
        work(p)
    for o in W_FAR:
        w_z[o].wait_recv()
        if o == 6:
            w_z[-6].wait_recv()
        over(-o)
    for p in range(7, 12):
        work(p)
    for p in range(12, 24):
        w_y[p - 12].wait_recv()
        work(p)

    gsum2[...] = fold(gram_w[0])
    cg_copy = send(gsum2.at[half_there], cgrecv, cg_s.at[0], cg_r.at[0], to_core)

    def column(dx, dy, core_):
        return acc[cols_tab[8, ((x + dx) % 4) * 8 + ((yh + dy) % 4) * 2 + core_]]

    y_order = (2, 1, 3, 0)
    c_copies = {}
    for dy in y_order:
        for dx in range(4):
            csend[dy, dx] = column(dx, dy, 1 - core)
        c_copies[dy] = send(csend.at[dy], crecv.at[dy], c_s.at[dy], c_r.at[dy], to_core)
    cg_copy.wait_recv()
    half_sum = gsum2[half_here, :] + cgrecv[...]
    ghalf[0] = half_sum
    gx = {d: send(ghalf.at[0], gxrecv.at[d - 1], gx_s.at[d - 1], gx_r.at[d - 1], to_x[d]) for d in (2, 1, 3)}
    x_copies = {}
    for dy in y_order:
        c_copies[dy].wait_recv()
        for dx in (2, 1, 3, 0):
            total = column(dx, dy, core) + crecv[dy, dx]
            if dx:
                n = (dx - 1) * 4 + dy
                xsend[n] = total
                x_copies[dx, dy] = send(xsend.at[n], xrecv.at[n], x_s.at[n], x_r.at[n], to_x[dx])
            else:
                own4[dy] = total
    drain(18)
    for d in (1, 3, 2):
        gx[d].wait_recv()
        half_sum = half_sum + gxrecv[d - 1]
    ghalf[1] = half_sum
    gy = {d: send(ghalf.at[1], gyrecv.at[d - 1], gy_s.at[d - 1], gy_r.at[d - 1], to_y[d]) for d in (2, 1, 3)}
    v_copies = {}
    for dy in y_order:
        cross = own4[dy]
        for dx in (1, 3, 2):
            x_copies[dx, dy].wait_recv()
            cross = cross + xrecv[(dx - 1) * 4 + dy]
        if dy:
            vsend[dy - 1] = cross
            v_copies[dy] = send(vsend.at[dy - 1], vrecv.at[dy - 1], v_s.at[dy - 1], v_r.at[dy - 1], to_y[dy])
    drain(6)
    for d in (1, 3, 2):
        gy[d].wait_recv()
        half_sum = half_sum + gyrecv[d - 1]
    ghalf[2] = half_sum
    gc = send(ghalf.at[2], ghalf.at[3], gc_s.at[0], gc_r.at[0], to_core)
    for d in (1, 3, 2):
        v_copies[d].wait_recv()
        cross = cross + vrecv[d - 1]
    gc.wait_recv()
    gram = joined(half_sum, ghalf[3])

    hals(unfold(gram), h_init, cross, h_out)
    drain()


def shards(tile_index, tile_values, w_init, h_init):
    dma = lambda n: pltpu.SemaphoreType.DMA((n,))
    vmem = pl.BlockSpec(memory_space=pltpu.VMEM)
    hbm = pl.BlockSpec(memory_space=pltpu.HBM)
    return pl.pallas_call(
        kernel,
        out_shape=(
            jax.ShapeDtypeStruct(w_init.shape, F32),
            jax.ShapeDtypeStruct(h_init.shape, F32),
        ),
        in_specs=[pl.BlockSpec(memory_space=pltpu.SMEM), hbm, hbm, hbm],
        out_specs=(vmem, vmem),
        scratch_shapes=[
            pltpu.VMEM((SLOTS, TILE, TILE), BF16),
            pltpu.VMEM((RANK, 2 * TILE), F32),
            pltpu.VMEM((RANK, TILE), F32),
            pltpu.VMEM((32, RANK, TILE), BF16),
            pltpu.VMEM((48, RANK, TILE), BF16),
            pltpu.VMEM((SLOTS + 1, RANK, TILE), F32),
            pltpu.VMEM((NZ, TILE, TILE), BF16),
            pltpu.VMEM((NZ, TILE, TILE), BF16),
            pltpu.VMEM((NZ - 1, TILE, TILE), BF16),
            pltpu.VMEM((NZ - 1, TILE, TILE), BF16),
            pltpu.VMEM((7, 16, TILE), F32),
            pltpu.VMEM((NZ - 1, 16, TILE), F32),
            pltpu.VMEM((4, 4, RANK, TILE), F32),
            pltpu.VMEM((4, 4, RANK, TILE), F32),
            pltpu.VMEM((12, RANK, TILE), F32),
            pltpu.VMEM((12, RANK, TILE), F32),
            pltpu.VMEM((3, RANK, TILE), F32),
            pltpu.VMEM((3, RANK, TILE), F32),
            pltpu.VMEM((4, RANK, TILE), F32),
            pltpu.VMEM((32, TILE), F32),
            pltpu.VMEM((32, TILE), F32),
            pltpu.VMEM((4, 16, TILE), F32),
            pltpu.VMEM((16, TILE), F32),
            pltpu.VMEM((3, 16, TILE), F32),
            pltpu.VMEM((3, 16, TILE), F32),
            pltpu.VMEM((2, 16, TILE), I32),
            pltpu.SMEM((16, TILE), I32),
            pltpu.SMEM((16, TILE), I32),
            dma(5), dma(3), dma(3), dma(12), dma(12), dma(16), dma(16),
            dma(NZ), dma(NZ), dma(13), dma(13), dma(NZ), dma(NZ),
            dma(NZ), dma(NZ), dma(NZ), dma(NZ), dma(4), dma(4), dma(1), dma(1),
            dma(3), dma(3), dma(3), dma(3), dma(1), dma(1), dma(12), dma(12), dma(3), dma(3),
        ],
        compiler_params=pltpu.CompilerParams(
            collective_id=0, has_side_effects=True, vmem_limit_bytes=20 * 2**20
        ),
        name="hals_sweep",
    )(
        tile_index.reshape(SLOTS),
        pltpu.with_memory_space_constraint(tile_values[0, 0], pltpu.HBM),
        pltpu.with_memory_space_constraint(w_init, pltpu.HBM),
        pltpu.with_memory_space_constraint(h_init, pltpu.HBM),
    )


def solution(mesh):
    in_specs = (
        P("user", "item", None),
        P("user", "item", None, None, None),
        P(None, ("user", "item")),
        P(None, ("item", "user")),
    )
    out_specs = (P(None, ("user", "item")), P(None, ("item", "user")))
    return jax.shard_map(shards, mesh=mesh, in_specs=in_specs, out_specs=out_specs, check_vma=False)
```
